512 devices in a mesh: seq: 32 (over x, z), chan: 16 (over y, core).
Axes of the slice: x: 4, y: 8, z: 8, core: 2. Of those that a mesh axis runs over, the one named last changes fastest.
Arguments:
- gate_input: bfloat16 [4096, 8192], P('chan', 'seq'), may hold values from -6 to 6
- key_input: bfloat16 [4096, 8192], P('chan', 'seq'), may hold values from -6 to 6
- value_input: bfloat16 [4096, 8192], P('chan', 'seq'), may hold values from -6 to 6
- short_taps: float32 [9, 4096], P(None, 'chan'), may hold values from -3.5 to 3.5
- skip_gain: float32 [4096], P('chan'), may hold values from -3 to 3
- decay_rates: float32 [4096, 16], P('chan'), may hold values from 6.1035156e-05 to 0.05
- residues: float32 [4096, 16], P('chan'), may hold values from -2 to 2
- out_weight: bfloat16 [4096, 4096], P('chan'), may hold values from -0.09375 to 0.09375
Outputs:
- output: bfloat16 [4096, 8192], P('chan', 'seq')
The draws below stay inside these ranges and needn't reach their ends.
All inputs are finite; a program needn't handle non-finite values.
Results may differ from the reference program's by a relative error of at most 0.0064.
Values may be sent and summed in bfloat16 or wider, within the bound.
A program may use at most 128 MiB of HBM per device.

```python
import math
import jax
import jax.numpy as jnp
from jax import lax

D = 4096
S = 16
TOKENS = 8192
N_CHAN = 16


def levels(stream_key, dims, cuts, smallest, top_value):
    gain, own = 1.0, jax.random.fold_in(stream_key, 6)
    for axis_at, blocks in cuts:
        heights = jnp.exp(jax.random.uniform(jax.random.fold_in(own, axis_at), (blocks,), jnp.float32, smallest / len(cuts), top_value / len(cuts)))
        gain = gain * jnp.repeat(heights, dims[axis_at] // blocks).reshape([-1 if axis == axis_at else 1 for axis in range(len(dims))])
    return gain


def scatter_about(key, dims, deviation, bound, cuts=(), held_as=jnp.bfloat16):
    values = jax.random.normal(key, dims, jnp.float32) * deviation
    if len(cuts) > 0:
        values = levels(key, dims, cuts, -0.22, 0.18) * values
    return jnp.clip(values, min=-bound, max=bound).astype(held_as)


def setup_inputs(seed: int = 0) -> dict:
    splits = jax.random.split(jax.random.key(seed), 9)
    return {
        "gate_input": scatter_about(splits[0], (D, TOKENS), 1.0, 6.0, ((0, 16), (1, 32))),
        "key_input": scatter_about(splits[1], (D, TOKENS), 1.0, 6.0, ((0, 16), (1, 32))),
        "value_input": scatter_about(splits[2], (D, TOKENS), 1.0, 6.0, ((0, 16), (1, 32))),
        "short_taps": scatter_about(splits[3], (9, D), 3 ** -0.5, 3.5, ((1, 16),), jnp.float32),
        "skip_gain": scatter_about(splits[4], (D,), 0.5, 3.0, ((0, 16),), jnp.float32),
        "decay_rates": jnp.clip(jnp.exp(math.log(0.05) - 6.7083283 * jax.random.uniform(splits[5], (D, S), jnp.float32) ** levels(splits[5], (D, S), ((0, 16),), -0.2, 0.2)), 6.103515625e-05, 0.05),
        "residues": scatter_about(splits[6], (D, S), 0.35, 2.0, ((0, 16),), jnp.float32),
        "out_weight": scatter_about(splits[7], (D, D), D ** -0.5, 0.09375, ((0, 16),)),
    }


def short_conv(signal, taps):
    wide = signal.astype(jnp.float32)
    result = taps[0][:, None] * wide
    for lag_steps in (1, 2):
        moved = jnp.pad(wide, ((0, 0), (lag_steps, 0)))[:, :wide.shape[1]]
        result = result + taps[lag_steps][:, None] * moved
    return result

def reference(gate_input, key_input, value_input, short_taps, skip_gain, decay_rates, residues, out_weight):
    block_size = D // N_CHAN
    block_count = D // block_size

    def per_block(pieces):
        gate_part, key_part, value_part, taps, gains, rates, weights_modes = pieces
        gate_short = short_conv(gate_part, taps[0:3])
        key_short = short_conv(key_part, taps[3:6])
        value_short = short_conv(value_part, taps[6:9])
        gated_input = (key_short * value_short).astype(jnp.bfloat16)
        positions = jnp.arange(TOKENS).astype(jnp.float32)
        filters = lax.optimization_barrier(jnp.sum(weights_modes[:, :, None] * jnp.sqrt(rates)[:, :, None] * jnp.exp(-rates[:, :, None] * positions[None, None, :]), axis=1))
        wide_input = gated_input.astype(jnp.float32)
        spectrum = jnp.fft.rfft(wide_input, n=2 * TOKENS, axis=1) * jnp.fft.rfft(filters, n=2 * TOKENS, axis=1)
        long_conv = jnp.fft.irfft(spectrum, n=2 * TOKENS, axis=1)[:, :TOKENS]
        mixed = (long_conv + gains[:, None] * wide_input).astype(jnp.bfloat16)
        mixed = lax.optimization_barrier(mixed)
        return (gate_short * mixed.astype(jnp.float32)).astype(jnp.bfloat16)
    stacked = (gate_input.reshape(block_count, block_size, TOKENS), key_input.reshape(block_count, block_size, TOKENS), value_input.reshape(block_count, block_size, TOKENS), jnp.transpose(short_taps.reshape(9, block_count, block_size), (1, 0, 2)), skip_gain.reshape(block_count, block_size), decay_rates.reshape(block_count, block_size, S), residues.reshape(block_count, block_size, S))
    gated = lax.map(per_block, stacked).reshape(D, TOKENS)
    return jnp.dot(out_weight, gated, preferred_element_type=jnp.float32).astype(jnp.bfloat16)
```

```python
import functools
import math

import jax
import jax.numpy as jnp
from jax import lax
from jax.experimental import pallas as pl
from jax.experimental.pallas import tpu as pltpu
from jax.sharding import PartitionSpec as P

MESH = pl.DeviceIdType.MESH
F32 = jnp.float32
BF16 = jnp.bfloat16
NZ = 8
MODES = 16
CHUNKS = 8
LANES = 128
MSG = 24


def rounded(value):
    return value.astype(BF16).astype(F32)


def kernel(
    nseq,
    nchan,
    gate_hbm,
    key_hbm,
    value_hbm,
    taps_ref,
    gain_ref,
    rates_ref,
    res_ref,
    weight_hbm,
    out_ref,
    gate_v,
    key_v,
    value_v,
    weight_v,
    perm,
    ext,
    u_ref,
    gs_ref,
    y_ref,
    gt_ref,
    a_rep,
    w_rep,
    cin,
    zbuf,
    xbuf,
    tmsg,
    gmsg,
    gbuf,
    carry,
    gathered,
    acc,
    in_sem,
    z_s,
    z_r,
    x_s,
    x_r,
    g_s,
    g_r,
    ring_s,
    ring_r,
    sib_s,
    sib_r,
):
    nx = nseq // NZ
    ny = nchan // 2
    half = ny // 2
    toks = gate_v.shape[1]
    chans = gate_v.shape[0]
    blocks = toks // CHUNKS
    halves = chans // LANES
    seq = lax.axis_index("seq")
    chan = lax.axis_index("chan")
    x, z = seq // NZ, seq % NZ
    y, core = chan // 2, chan % 2
    sibling = chan + 1 - 2 * core

    loads = []
    for n, (src, dst) in enumerate(
        ((key_hbm, key_v), (value_hbm, value_v), (gate_hbm, gate_v), (weight_hbm, weight_v))
    ):
        copy = pltpu.make_async_copy(src, dst, in_sem.at[n])
        copy.start()
        loads.append(copy)

    z_peers = [x * NZ + (z + d) % NZ for d in range(1, NZ)]
    x_peers = [((x + d) % nx) * NZ + z for d in range(1, nx)]
    after, before = (seq + 1) % nseq, (seq + nseq - 1) % nseq
    above = ((y + 1) % ny) * 2 + core
    below = ((y + ny - 1) % ny) * 2 + core

    barrier = pltpu.get_barrier_semaphore()
    peers = [(s, chan) for s in z_peers + x_peers + [after, before]]
    peers += [(seq, c) for c in (above, below, sibling)]
    for peer in peers:
        pl.semaphore_signal(barrier, inc=1, device_id=peer, device_id_type=MESH)

    row = lax.broadcasted_iota(jnp.int32, (toks, toks), 0)
    col = lax.broadcasted_iota(jnp.int32, (toks, toks), 1)
    perm[...] = jnp.where(col == (row % CHUNKS) * blocks + row // CHUNKS, 1.0, 0.0).astype(BF16)

    def nt(lhs, rhs, precision=None):
        return lax.dot_general(
            lhs, rhs, (((1,), (1,)), ((), ())), precision=precision, preferred_element_type=F32
        )

    pick_rep = jnp.where(
        lax.broadcasted_iota(jnp.int32, (MODES * CHUNKS, MODES), 0) // CHUNKS
        == lax.broadcasted_iota(jnp.int32, (MODES * CHUNKS, MODES), 1),
        1.0,
        0.0,
    )
    pick = jnp.where(
        lax.broadcasted_iota(jnp.int32, (MODES, MODES), 0)
        == lax.broadcasted_iota(jnp.int32, (MODES, MODES), 1),
        1.0,
        0.0,
    )
    rates = rates_ref[...]
    weights = res_ref[...] * jnp.sqrt(rates)
    high = lax.Precision.HIGHEST
    r_rep = nt(pick_rep, rates, high)
    a_rep[...] = jnp.exp(-r_rep).reshape(MODES, CHUNKS, chans)
    w_rep[...] = nt(pick_rep, weights, high).reshape(MODES, CHUNKS, chans)
    r_c = nt(pick, rates, high)
    w_c = nt(pick, weights, high)

    first = lax.broadcasted_iota(jnp.int32, (CHUNKS, chans), 0) == 0
    tail = CHUNKS * (blocks - 2)

    def short(which, source):
        loads[which].wait()
        laid = nt(perm[...], source[...])
        m = (1, 2, 0)[which]
        tap = [taps_ref[3 * m + j : 3 * m + j + 1, :] for j in range(3)]
        ext[2 * CHUNKS :, :] = laid
        for n in range(2):
            block = laid[tail + n * CHUNKS : tail + (n + 1) * CHUNKS]
            ext[n * CHUNKS : (n + 1) * CHUNKS, :] = jnp.where(first, 0.0, pltpu.roll(block, 1, 0))
        result = tap[0] * laid
        result = result + tap[1] * ext[CHUNKS : CHUNKS + toks, :]
        result = result + tap[2] * ext[0:toks, :]
        last = laid[toks - 1 : toks]
        prev = laid[toks - 1 - CHUNKS : toks - CHUNKS]
        return result, tap[1] * last + tap[2] * prev, tap[2] * last

    own = zbuf.at[z]
    key_short, q0, q1 = short(0, key_v)
    own[16:17, :] = key_short[0:1]
    own[17:18, :] = key_short[CHUNKS : CHUNKS + 1]
    own[20:21, :] = q0
    own[21:22, :] = q1
    value_short, q0, q1 = short(1, value_v)
    own[18:19, :] = value_short[0:1]
    own[19:20, :] = value_short[CHUNKS : CHUNKS + 1]
    own[22:23, :] = q0
    own[23:24, :] = q1
    u_ref[...] = rounded(key_short * value_short)
    for n in range(2):
        u_ref[n * CHUNKS : n * CHUNKS + 1, :] = jnp.zeros((1, chans), F32)

    k3 = lax.broadcasted_iota(jnp.int32, (MODES, CHUNKS, LANES), 1)
    for h in range(halves):
        lanes = slice(h * LANES, (h + 1) * LANES)
        a = a_rep[:, :, lanes]

        def scan(i, state):
            u = u_ref[pl.ds(pl.multiple_of(i * CHUNKS, CHUNKS), CHUNKS), lanes]
            return state * a + u[None]

        state = lax.fori_loop(0, blocks, scan, jnp.zeros((MODES, CHUNKS, LANES), F32), unroll=8)
        step = a
        for _ in range(int(math.log2(blocks))):
            step = step * step
        shift = 1
        while shift < CHUNKS:
            moved = jnp.where(k3 >= shift, pltpu.roll(state, shift, 1), 0.0)
            state = state + step * moved
            step = step * step
            shift *= 2
        cin[:, :, lanes] = jnp.where(k3 >= 1, pltpu.roll(state, 1, 1), 0.0)
        for s in range(MODES):
            own[s : s + 1, lanes] = state[s, CHUNKS - 1 : CHUNKS, :]

    pl.semaphore_wait(barrier, len(peers))

    def send(src, dst, ssem, rsem, peer):
        copy = pltpu.make_async_remote_copy(
            src_ref=src,
            dst_ref=dst,
            send_sem=ssem,
            recv_sem=rsem,
            device_id=peer,
            device_id_type=MESH,
        )
        copy.start()
        return copy

    sent = []
    for n, peer in enumerate(z_peers):
        sent.append(send(own, own, z_s.at[n], z_r.at[n], (peer, chan)))

    gate_short, q0, q1 = short(2, gate_v)
    gs_ref[...] = gate_short
    gmsg[...] = jnp.zeros_like(gmsg)
    gmsg[0:1, :] = q0
    gmsg[1:2, :] = q1
    sent.append(send(gmsg, gbuf, g_s.at[0], g_r.at[0], (after, chan)))

    for h in range(halves):
        lanes = slice(h * LANES, (h + 1) * LANES)
        a = a_rep[:, :, lanes]
        w = w_rep[:, :, lanes]

        def local(i, state):
            rows = pl.ds(pl.multiple_of(i * CHUNKS, CHUNKS), CHUNKS)
            state = state * a + u_ref[rows, lanes][None]
            y_ref[rows, lanes] = jnp.sum(state * w, axis=0)
            return state

        lax.fori_loop(0, blocks, local, jnp.zeros((MODES, CHUNKS, LANES), F32), unroll=4)

    def decay(count):
        return jnp.exp(-r_c * count)

    def edge_tokens(q, msg):
        u0 = rounded((msg[16:17] + q[0:1]) * (msg[18:19] + q[2:3]))
        u1 = rounded((msg[17:18] + q[1:2]) * (msg[19:20] + q[3:4]))
        return u0, u1

    def arrival(buf, index, rsem):
        return pltpu.make_async_remote_copy(
            src_ref=buf.at[index],
            dst_ref=buf.at[index],
            send_sem=z_s.at[0],
            recv_sem=rsem,
            device_id=(seq, chan),
            device_id_type=MESH,
        )

    span = float(toks)
    d0, d1, d2 = decay(span), decay(span - 1.0), decay(span - 2.0)
    e0, e1, e2 = decay(NZ * span), decay(NZ * span - 1.0), decay(NZ * span - 2.0)
    for n in range(NZ - 1):
        arrival(zbuf, (z + NZ - 1 - n) % NZ, z_r.at[n]).wait_recv()
    msg = zbuf[0]
    cur, q = msg[:MODES], msg[20:24]
    zero = jnp.zeros((MODES, chans), F32)
    mine, mine_q = zero, jnp.zeros((4, chans), F32)
    for n in range(1, NZ):
        here = z == n
        mine = jnp.where(here, cur, mine)
        mine_q = jnp.where(here, q, mine_q)
        msg = zbuf[n]
        u0, u1 = edge_tokens(q, msg)
        cur = d0 * cur + msg[:MODES] + d1 * u0 + d2 * u1
        q = msg[20:24]
    tmsg[0:MODES, :] = cur
    tmsg[16:20, :] = zbuf[0, 16:20, :]
    tmsg[20:24, :] = q
    for n, peer in enumerate(x_peers):
        sent.append(send(tmsg, xbuf.at[x], x_s.at[n], x_r.at[n], (peer, chan)))

    for n in range(nx - 1):
        arrival(xbuf, (x + nx - 1 - n) % nx, x_r.at[n]).wait_recv()
    cur, q = zero, jnp.zeros((4, chans), F32)
    for n in range(nx - 1):
        use = n < x
        msg = xbuf[n]
        u0, u1 = edge_tokens(q, msg)
        new = e0 * cur + msg[:MODES] + e1 * u0 + e2 * u1
        cur = jnp.where(use, new, cur)
        q = jnp.where(use, msg[20:24], q)
    u0, u1 = edge_tokens(q, zbuf[0])
    ahead = z.astype(F32) * span
    inside = mine + decay(ahead) * cur + decay(ahead - 1.0) * u0 + decay(ahead - 2.0) * u1
    at_first = z == 0
    state_in = jnp.where(at_first, cur, inside)
    q = jnp.where(at_first, q, mine_q)
    u0, u1 = edge_tokens(q, own)
    u_ref[0:1, :] = u0
    u_ref[CHUNKS : CHUNKS + 1, :] = u1
    back = jnp.exp(r_c)
    carry[...] = state_in + back * u0 + back * back * u1
    y_ref[0:1, :] = y_ref[0:1, :] - jnp.sum(w_c * back, axis=0, keepdims=True) * u1
    pltpu.make_async_remote_copy(
        src_ref=gmsg,
        dst_ref=gbuf,
        send_sem=g_s.at[0],
        recv_sem=g_r.at[0],
        device_id=(seq, chan),
        device_id_type=MESH,
    ).wait_recv()
    begins = seq == 0
    for n in range(2):
        at = slice(n * CHUNKS, n * CHUNKS + 1)
        gs_ref[at, :] = gs_ref[at, :] + jnp.where(begins, 0.0, gbuf[n : n + 1, :])

    def piece_of(c, h):
        return gathered.at[c, pl.ds(h * LANES, LANES)]

    def goes(way, hop, h):
        return hop < half or (hop == half and h % 2 == way)

    def forward(way, hop, h, c):
        block = piece_of(c, h)
        peer = (seq, (above, below)[way])
        sem = (way, hop - 1, h)
        sent.append(send(block, block, ring_s.at[sem], ring_r.at[sem], peer))

    def share(slot, h, c):
        block = piece_of(c, h)
        sem = (slot, h)
        sent.append(send(block, block, sib_s.at[sem], sib_r.at[sem], (seq, sibling)))

    def wait_block(c, h, rsem):
        block = piece_of(c, h)
        pltpu.make_async_remote_copy(
            src_ref=block,
            dst_ref=block,
            send_sem=z_s.at[0],
            recv_sem=rsem,
            device_id=(seq, chan),
            device_id_type=MESH,
        ).wait_recv()

    k8 = lax.broadcasted_iota(jnp.int32, (CHUNKS, LANES), 0).astype(F32) * float(blocks)
    for h in range(halves):
        lanes = slice(h * LANES, (h + 1) * LANES)
        a = a_rep[:, :, lanes]
        lead = jnp.stack(
            [
                jnp.broadcast_to(carry[s : s + 1, lanes], (CHUNKS, LANES))
                * jnp.exp(-jnp.broadcast_to(r_c[s : s + 1, lanes], (CHUNKS, LANES)) * k8)
                for s in range(MODES)
            ]
        )
        start = w_rep[:, :, lanes] * a * (lead + cin[:, :, lanes])
        gain = gain_ref[:, lanes]

        def finish(i, state):
            rows = pl.ds(pl.multiple_of(i * CHUNKS, CHUNKS), CHUNKS)
            conv = y_ref[rows, lanes] + jnp.sum(state, axis=0)
            mixed = rounded(conv + gain * u_ref[rows, lanes])
            gt_ref[rows, :] = gs_ref[rows, lanes] * mixed
            return state * a

        lax.fori_loop(0, blocks, finish, start, unroll=4)
        gathered[chan, h * LANES : (h + 1) * LANES, :] = lax.dot_general(
            gt_ref[...].astype(BF16),
            perm[...],
            (((0,), (0,)), ((), ())),
            preferred_element_type=F32,
        ).astype(BF16)
        for way in range(2):
            if goes(way, 1, h):
                forward(way, 1, h, chan)
        share(0, h, chan)

    loads[3].wait()

    def product(c):
        cols = pl.ds(pl.multiple_of(c * chans, chans), chans)
        return jnp.dot(weight_v[:, cols], gathered[c], preferred_element_type=F32)

    def other(c):
        return c + 1 - 2 * core

    acc[...] = product(chan)
    for h in range(halves):
        wait_block(sibling, h, sib_r.at[0, h])
    acc[...] += product(sibling)
    for hop in range(1, half + 1):
        origins = [((y + ny - hop) % ny) * 2 + core, ((y + hop) % ny) * 2 + core]
        for h in range(halves):
            for way in range(2):
                if goes(way, hop, h):
                    c = origins[way]
                    wait_block(c, h, ring_r.at[way, hop - 1, h])
                    if goes(way, hop + 1, h):
                        forward(way, hop + 1, h, c)
                    share(1 + way * half + hop - 1, h, c)
        arrived = origins if hop < half else origins[:1]
        total = product(arrived[0])
        for c in arrived[1:]:
            total += product(c)
        acc[...] += total
        for h in range(halves):
            for way in range(2):
                if goes(way, hop, h):
                    wait_block(other(origins[way]), h, sib_r.at[1 + way * half + hop - 1, h])
        total = product(other(arrived[0]))
        for c in arrived[1:]:
            total += product(other(c))
        if hop < half:
            acc[...] += total
        else:
            out_ref[...] = (acc[...] + total).astype(BF16)
    for copy in sent:
        copy.wait_send()


def body(nseq, nchan, gate, key, value, taps, gain, rates, residues, weight):
    chans, toks = gate.shape
    half = nchan // 4
    vmem = pl.BlockSpec(memory_space=pltpu.VMEM)
    anywhere = pl.BlockSpec(memory_space=pl.ANY)
    dma = pltpu.SemaphoreType.DMA
    nx = nseq // NZ
    return pl.pallas_call(
        functools.partial(kernel, nseq, nchan),
        out_shape=jax.ShapeDtypeStruct((weight.shape[0], toks), BF16),
        in_specs=[anywhere] * 3 + [vmem] * 4 + [anywhere],
        out_specs=vmem,
        scratch_shapes=[
            pltpu.VMEM((chans, toks), BF16),
            pltpu.VMEM((chans, toks), BF16),
            pltpu.VMEM((chans, toks), BF16),
            pltpu.VMEM(weight.shape, BF16),
            pltpu.VMEM((toks, toks), BF16),
            pltpu.VMEM((toks + 2 * CHUNKS, chans), F32),
            pltpu.VMEM((toks, chans), F32),
            pltpu.VMEM((toks, chans), F32),
            pltpu.VMEM((toks, chans), F32),
            pltpu.VMEM((toks, LANES), F32),
            pltpu.VMEM((MODES, CHUNKS, chans), F32),
            pltpu.VMEM((MODES, CHUNKS, chans), F32),
            pltpu.VMEM((MODES, CHUNKS, chans), F32),
            pltpu.VMEM((NZ, MSG, chans), F32),
            pltpu.VMEM((nx, MSG, chans), F32),
            pltpu.VMEM((MSG, chans), F32),
            pltpu.VMEM((8, chans), F32),
            pltpu.VMEM((8, chans), F32),
            pltpu.VMEM((MODES, chans), F32),
            pltpu.VMEM((nchan, chans, toks), BF16),
            pltpu.VMEM((weight.shape[0], toks), F32),
            dma((4,)),
            dma((NZ - 1,)),
            dma((NZ - 1,)),
            dma((max(nx - 1, 1),)),
            dma((max(nx - 1, 1),)),
            dma((1,)),
            dma((1,)),
            dma((2, half, 2)),
            dma((2, half, 2)),
            dma((1 + 2 * half, 2)),
            dma((1 + 2 * half, 2)),
        ],
        compiler_params=pltpu.CompilerParams(
            collective_id=0, has_side_effects=True, vmem_limit_bytes=40 * 1024 * 1024
        ),
        name="hyena",
    )(gate, key, value, taps, gain.reshape(1, -1), rates, residues, weight)


def solution(mesh):
    in_specs = (
        P("chan", "seq"),
        P("chan", "seq"),
        P("chan", "seq"),
        P(None, "chan"),
        P("chan"),
        P("chan", None),
        P("chan", None),
        P("chan", None),
    )
    return jax.shard_map(
        functools.partial(body, mesh.shape["seq"], mesh.shape["chan"]),
        mesh=mesh,
        in_specs=in_specs,
        out_specs=P("chan", "seq"),
        check_vma=False,
    )
```

```python
import functools
import math

import jax
import jax.numpy as jnp
from jax import lax
from jax.experimental import pallas as pl
from jax.experimental.pallas import tpu as pltpu
from jax.sharding import PartitionSpec as P

MESH = pl.DeviceIdType.MESH
F32 = jnp.float32
BF16 = jnp.bfloat16
NZ = 8
MODES = 16
CHUNKS = 8
LANES = 128
MSG = 24


def rounded(value):
    return value.astype(BF16).astype(F32)


def kernel(
    nseq,
    nchan,
    gate_hbm,
    key_hbm,
    value_hbm,
    taps_hbm,
    gain_hbm,
    rates_hbm,
    res_hbm,
    weight_hbm,
    out_ref,
    taps_v,
    gain_v,
    rates_v,
    res_v,
    gate_v,
    key_v,
    value_v,
    weight_v,
    perm,
    ext,
    u_ref,
    gs_ref,
    y_ref,
    gt_ref,
    a_rep,
    w_rep,
    cin,
    zbuf,
    xbuf,
    tmsg,
    gmsg,
    gbuf,
    carry,
    gathered,
    acc,
    in_sem,
    z_s,
    z_r,
    x_s,
    x_r,
    g_s,
    g_r,
    ring_s,
    ring_r,
    sib_s,
    sib_r,
):
    nx = nseq // NZ
    ny = nchan // 2
    half = ny // 2
    toks = gate_v.shape[1]
    chans = gate_v.shape[0]
    blocks = toks // CHUNKS
    halves = chans // LANES
    seq = lax.axis_index("seq")
    chan = lax.axis_index("chan")
    x, z = seq // NZ, seq % NZ
    y, core = chan // 2, chan % 2
    sibling = chan + 1 - 2 * core

    loads = []
    for n, (src, dst) in enumerate(
        (
            (rates_hbm, rates_v),
            (res_hbm, res_v),
            (taps_hbm, taps_v),
            (key_hbm, key_v),
            (value_hbm, value_v),
            (gate_hbm, gate_v),
            (gain_hbm, gain_v),
            (weight_hbm, weight_v),
        )
    ):
        copy = pltpu.make_async_copy(src, dst, in_sem.at[n])
        copy.start()
        loads.append(copy)

    z_peers = [x * NZ + (z + d) % NZ for d in range(1, NZ)]
    x_peers = [((x + d) % nx) * NZ + z for d in range(1, nx)]
    after, before = (seq + 1) % nseq, (seq + nseq - 1) % nseq
    above = ((y + 1) % ny) * 2 + core
    below = ((y + ny - 1) % ny) * 2 + core

    barrier = pltpu.get_barrier_semaphore()
    peers = [(s, chan) for s in z_peers + x_peers + [after, before]]
    peers += [(seq, c) for c in (above, below, sibling)]
    for peer in peers:
        pl.semaphore_signal(barrier, inc=1, device_id=peer, device_id_type=MESH)

    row = lax.broadcasted_iota(jnp.int32, (toks, toks), 0)
    col = lax.broadcasted_iota(jnp.int32, (toks, toks), 1)
    perm[...] = jnp.where(col == (row % CHUNKS) * blocks + row // CHUNKS, 1.0, 0.0).astype(BF16)

    def nt(lhs, rhs, precision=None):
        return lax.dot_general(
            lhs, rhs, (((1,), (1,)), ((), ())), precision=precision, preferred_element_type=F32
        )

    loads[0].wait()
    loads[1].wait()
    r_c = rates_v[...]
    w_c = res_v[...] * jnp.sqrt(r_c)
    a_c = jnp.exp(-r_c)
    for s in range(MODES):
        a_rep[s] = jnp.broadcast_to(a_c[s : s + 1], (CHUNKS, chans))
        w_rep[s] = jnp.broadcast_to(w_c[s : s + 1], (CHUNKS, chans))

    first = lax.broadcasted_iota(jnp.int32, (CHUNKS, chans), 0) == 0
    tail = CHUNKS * (blocks - 2)

    loads[2].wait()

    def short(which, source):
        loads[3 + which].wait()
        laid = nt(perm[...], source[...])
        m = (1, 2, 0)[which]
        tap = [taps_v[3 * m + j : 3 * m + j + 1, :] for j in range(3)]
        ext[2 * CHUNKS :, :] = laid
        for n in range(2):
            block = laid[tail + n * CHUNKS : tail + (n + 1) * CHUNKS]
            ext[n * CHUNKS : (n + 1) * CHUNKS, :] = jnp.where(first, 0.0, pltpu.roll(block, 1, 0))
        result = tap[0] * laid
        result = result + tap[1] * ext[CHUNKS : CHUNKS + toks, :]
        result = result + tap[2] * ext[0:toks, :]
        last = laid[toks - 1 : toks]
        prev = laid[toks - 1 - CHUNKS : toks - CHUNKS]
        return result, tap[1] * last + tap[2] * prev, tap[2] * last

    own = zbuf.at[z]
    key_short, q0, q1 = short(0, key_v)
    own[16:17, :] = key_short[0:1]
    own[17:18, :] = key_short[CHUNKS : CHUNKS + 1]
    own[20:21, :] = q0
    own[21:22, :] = q1
    value_short, q0, q1 = short(1, value_v)
    own[18:19, :] = value_short[0:1]
    own[19:20, :] = value_short[CHUNKS : CHUNKS + 1]
    own[22:23, :] = q0
    own[23:24, :] = q1
    u_ref[...] = rounded(key_short * value_short)
    for n in range(2):
        u_ref[n * CHUNKS : n * CHUNKS + 1, :] = jnp.zeros((1, chans), F32)

    k3 = lax.broadcasted_iota(jnp.int32, (MODES, CHUNKS, LANES), 1)
    for h in range(halves):
        lanes = slice(h * LANES, (h + 1) * LANES)
        a = a_rep[:, :, lanes]

        def scan(i, state):
            u = u_ref[pl.ds(pl.multiple_of(i * CHUNKS, CHUNKS), CHUNKS), lanes]
            return state * a + u[None]

        state = lax.fori_loop(0, blocks, scan, jnp.zeros((MODES, CHUNKS, LANES), F32), unroll=8)
        step = a
        for _ in range(int(math.log2(blocks))):
            step = step * step
        shift = 1
        while shift < CHUNKS:
            moved = jnp.where(k3 >= shift, pltpu.roll(state, shift, 1), 0.0)
            state = state + step * moved
            step = step * step
            shift *= 2
        cin[:, :, lanes] = jnp.where(k3 >= 1, pltpu.roll(state, 1, 1), 0.0)
        for s in range(MODES):
            own[s : s + 1, lanes] = state[s, CHUNKS - 1 : CHUNKS, :]

    pl.semaphore_wait(barrier, len(peers))

    def send(src, dst, ssem, rsem, peer):
        copy = pltpu.make_async_remote_copy(
            src_ref=src,
            dst_ref=dst,
            send_sem=ssem,
            recv_sem=rsem,
            device_id=peer,
            device_id_type=MESH,
        )
        copy.start()
        return copy

    sent = []
    for n, peer in enumerate(z_peers):
        sent.append(send(own, own, z_s.at[n], z_r.at[n], (peer, chan)))

    gate_short, q0, q1 = short(2, gate_v)
    gs_ref[...] = gate_short
    gmsg[...] = jnp.zeros_like(gmsg)
    gmsg[0:1, :] = q0
    gmsg[1:2, :] = q1
    sent.append(send(gmsg, gbuf, g_s.at[0], g_r.at[0], (after, chan)))

    for h in range(halves):
        lanes = slice(h * LANES, (h + 1) * LANES)
        a = a_rep[:, :, lanes]
        w = w_rep[:, :, lanes]

        def local(i, state):
            rows = pl.ds(pl.multiple_of(i * CHUNKS, CHUNKS), CHUNKS)
            state = state * a + u_ref[rows, lanes][None]
            y_ref[rows, lanes] = jnp.sum(state * w, axis=0)
            return state

        lax.fori_loop(0, blocks, local, jnp.zeros((MODES, CHUNKS, LANES), F32), unroll=4)

    def decay(count):
        return jnp.exp(-r_c * count)

    def edge_tokens(q, msg):
        u0 = rounded((msg[16:17] + q[0:1]) * (msg[18:19] + q[2:3]))
        u1 = rounded((msg[17:18] + q[1:2]) * (msg[19:20] + q[3:4]))
        return u0, u1

    def arrival(buf, index, rsem):
        return pltpu.make_async_remote_copy(
            src_ref=buf.at[index],
            dst_ref=buf.at[index],
            send_sem=z_s.at[0],
            recv_sem=rsem,
            device_id=(seq, chan),
            device_id_type=MESH,
        )

    span = float(toks)
    d0, d1, d2 = decay(span), decay(span - 1.0), decay(span - 2.0)
    e0, e1, e2 = decay(NZ * span), decay(NZ * span - 1.0), decay(NZ * span - 2.0)
    for n in range(NZ - 1):
        arrival(zbuf, (z + NZ - 1 - n) % NZ, z_r.at[n]).wait_recv()
    msg = zbuf[0]
    cur, q = msg[:MODES], msg[20:24]
    zero = jnp.zeros((MODES, chans), F32)
    mine, mine_q = zero, jnp.zeros((4, chans), F32)
    for n in range(1, NZ):
        here = z == n
        mine = jnp.where(here, cur, mine)
        mine_q = jnp.where(here, q, mine_q)
        msg = zbuf[n]
        u0, u1 = edge_tokens(q, msg)
        cur = d0 * cur + msg[:MODES] + d1 * u0 + d2 * u1
        q = msg[20:24]
    tmsg[0:MODES, :] = cur
    tmsg[16:20, :] = zbuf[0, 16:20, :]
    tmsg[20:24, :] = q
    for n, peer in enumerate(x_peers):
        sent.append(send(tmsg, xbuf.at[x], x_s.at[n], x_r.at[n], (peer, chan)))

    for n in range(nx - 1):
        arrival(xbuf, (x + nx - 1 - n) % nx, x_r.at[n]).wait_recv()
    cur, q = zero, jnp.zeros((4, chans), F32)
    for n in range(nx - 1):
        use = n < x
        msg = xbuf[n]
        u0, u1 = edge_tokens(q, msg)
        new = e0 * cur + msg[:MODES] + e1 * u0 + e2 * u1
        cur = jnp.where(use, new, cur)
        q = jnp.where(use, msg[20:24], q)
    u0, u1 = edge_tokens(q, zbuf[0])
    ahead = z.astype(F32) * span
    inside = mine + decay(ahead) * cur + decay(ahead - 1.0) * u0 + decay(ahead - 2.0) * u1
    at_first = z == 0
    state_in = jnp.where(at_first, cur, inside)
    q = jnp.where(at_first, q, mine_q)
    u0, u1 = edge_tokens(q, own)
    u_ref[0:1, :] = u0
    u_ref[CHUNKS : CHUNKS + 1, :] = u1
    back = jnp.exp(r_c)
    carry[...] = state_in + back * u0 + back * back * u1
    y_ref[0:1, :] = y_ref[0:1, :] - jnp.sum(w_c * back, axis=0, keepdims=True) * u1
    pltpu.make_async_remote_copy(
        src_ref=gmsg,
        dst_ref=gbuf,
        send_sem=g_s.at[0],
        recv_sem=g_r.at[0],
        device_id=(seq, chan),
        device_id_type=MESH,
    ).wait_recv()
    begins = seq == 0
    for n in range(2):
        at = slice(n * CHUNKS, n * CHUNKS + 1)
        gs_ref[at, :] = gs_ref[at, :] + jnp.where(begins, 0.0, gbuf[n : n + 1, :])

    def piece_of(c, h):
        return gathered.at[c, pl.ds(h * LANES, LANES)]

    def goes(way, hop, h):
        return hop < half or (hop == half and h % 2 == way)

    def forward(way, hop, h, c):
        block = piece_of(c, h)
        peer = (seq, (above, below)[way])
        sem = (way, hop - 1, h)
        sent.append(send(block, block, ring_s.at[sem], ring_r.at[sem], peer))

    def share(slot, h, c):
        block = piece_of(c, h)
        sem = (slot, h)
        sent.append(send(block, block, sib_s.at[sem], sib_r.at[sem], (seq, sibling)))

    def wait_block(c, h, rsem):
        block = piece_of(c, h)
        pltpu.make_async_remote_copy(
            src_ref=block,
            dst_ref=block,
            send_sem=z_s.at[0],
            recv_sem=rsem,
            device_id=(seq, chan),
            device_id_type=MESH,
        ).wait_recv()

    loads[6].wait()
    k8 = lax.broadcasted_iota(jnp.int32, (CHUNKS, LANES), 0).astype(F32) * float(blocks)
    for h in range(halves):
        lanes = slice(h * LANES, (h + 1) * LANES)
        a = a_rep[:, :, lanes]
        lead = jnp.stack(
            [
                jnp.broadcast_to(carry[s : s + 1, lanes], (CHUNKS, LANES))
                * jnp.exp(-jnp.broadcast_to(r_c[s : s + 1, lanes], (CHUNKS, LANES)) * k8)
                for s in range(MODES)
            ]
        )
        start = w_rep[:, :, lanes] * a * (lead + cin[:, :, lanes])
        gain = gain_v[:, lanes]

        def finish(i, state):
            rows = pl.ds(pl.multiple_of(i * CHUNKS, CHUNKS), CHUNKS)
            conv = y_ref[rows, lanes] + jnp.sum(state, axis=0)
            mixed = rounded(conv + gain * u_ref[rows, lanes])
            gt_ref[rows, :] = gs_ref[rows, lanes] * mixed
            return state * a

        lax.fori_loop(0, blocks, finish, start, unroll=4)
        gathered[chan, h * LANES : (h + 1) * LANES, :] = lax.dot_general(
            gt_ref[...].astype(BF16),
            perm[...],
            (((0,), (0,)), ((), ())),
            preferred_element_type=F32,
        ).astype(BF16)
        for way in range(2):
            if goes(way, 1, h):
                forward(way, 1, h, chan)
        share(0, h, chan)

    loads[7].wait()

    def product(c):
        cols = pl.ds(pl.multiple_of(c * chans, chans), chans)
        return jnp.dot(weight_v[:, cols], gathered[c], preferred_element_type=F32)

    def other(c):
        return c + 1 - 2 * core

    acc[...] = product(chan)
    for h in range(halves):
        wait_block(sibling, h, sib_r.at[0, h])
    acc[...] += product(sibling)
    for hop in range(1, half + 1):
        origins = [((y + ny - hop) % ny) * 2 + core, ((y + hop) % ny) * 2 + core]
        for h in range(halves):
            for way in range(2):
                if goes(way, hop, h):
                    c = origins[way]
                    wait_block(c, h, ring_r.at[way, hop - 1, h])
                    if goes(way, hop + 1, h):
                        forward(way, hop + 1, h, c)
                    share(1 + way * half + hop - 1, h, c)
        arrived = origins if hop < half else origins[:1]
        total = product(arrived[0])
        for c in arrived[1:]:
            total += product(c)
        acc[...] += total
        for h in range(halves):
            for way in range(2):
                if goes(way, hop, h):
                    wait_block(other(origins[way]), h, sib_r.at[1 + way * half + hop - 1, h])
        total = product(other(arrived[0]))
        for c in arrived[1:]:
            total += product(other(c))
        if hop < half:
            acc[...] += total
        else:
            out_ref[...] = (acc[...] + total).astype(BF16)
    for copy in sent:
        copy.wait_send()


def body(nseq, nchan, gate, key, value, taps, gain, rates, residues, weight):
    chans, toks = gate.shape
    half = nchan // 4
    vmem = pl.BlockSpec(memory_space=pltpu.VMEM)
    anywhere = pl.BlockSpec(memory_space=pl.ANY)
    dma = pltpu.SemaphoreType.DMA
    nx = nseq // NZ
    return pl.pallas_call(
        functools.partial(kernel, nseq, nchan),
        out_shape=jax.ShapeDtypeStruct((weight.shape[0], toks), BF16),
        in_specs=[anywhere] * 8,
        out_specs=vmem,
        scratch_shapes=[
            pltpu.VMEM(taps.shape, F32),
            pltpu.VMEM((1, chans), F32),
            pltpu.VMEM((MODES, chans), F32),
            pltpu.VMEM((MODES, chans), F32),
            pltpu.VMEM((chans, toks), BF16),
            pltpu.VMEM((chans, toks), BF16),
            pltpu.VMEM((chans, toks), BF16),
            pltpu.VMEM(weight.shape, BF16),
            pltpu.VMEM((toks, toks), BF16),
            pltpu.VMEM((toks + 2 * CHUNKS, chans), F32),
            pltpu.VMEM((toks, chans), F32),
            pltpu.VMEM((toks, chans), F32),
            pltpu.VMEM((toks, chans), F32),
            pltpu.VMEM((toks, LANES), F32),
            pltpu.VMEM((MODES, CHUNKS, chans), F32),
            pltpu.VMEM((MODES, CHUNKS, chans), F32),
            pltpu.VMEM((MODES, CHUNKS, chans), F32),
            pltpu.VMEM((NZ, MSG, chans), F32),
            pltpu.VMEM((nx, MSG, chans), F32),
            pltpu.VMEM((MSG, chans), F32),
            pltpu.VMEM((8, chans), F32),
            pltpu.VMEM((8, chans), F32),
            pltpu.VMEM((MODES, chans), F32),
            pltpu.VMEM((nchan, chans, toks), BF16),
            pltpu.VMEM((weight.shape[0], toks), F32),
            dma((8,)),
            dma((NZ - 1,)),
            dma((NZ - 1,)),
            dma((max(nx - 1, 1),)),
            dma((max(nx - 1, 1),)),
            dma((1,)),
            dma((1,)),
            dma((2, half, 2)),
            dma((2, half, 2)),
            dma((1 + 2 * half, 2)),
            dma((1 + 2 * half, 2)),
        ],
        compiler_params=pltpu.CompilerParams(
            collective_id=0, has_side_effects=True, vmem_limit_bytes=62 * 1024 * 1024
        ),
        name="hyena",
    )(gate, key, value, taps, gain.reshape(1, -1), rates.T, residues.T, weight)


def solution(mesh):
    in_specs = (
        P("chan", "seq"),
        P("chan", "seq"),
        P("chan", "seq"),
        P(None, "chan"),
        P("chan"),
        P("chan", None),
        P("chan", None),
        P("chan", None),
    )
    return jax.shard_map(
        functools.partial(body, mesh.shape["seq"], mesh.shape["chan"]),
        mesh=mesh,
        in_specs=in_specs,
        out_specs=P("chan", "seq"),
        check_vma=False,
    )
```

```python
import functools
import math

import jax
import jax.numpy as jnp
from jax import lax
from jax.experimental import pallas as pl
from jax.experimental.pallas import tpu as pltpu
from jax.sharding import PartitionSpec as P

MESH = pl.DeviceIdType.MESH
F32 = jnp.float32
BF16 = jnp.bfloat16
NZ = 8
MODES = 16
CHUNKS = 8
LANES = 128
MSG = 32
LATE = 24


def rounded(value):
    return value.astype(BF16).astype(F32)


def nt(lhs, rhs):
    return lax.dot_general(lhs, rhs, (((1,), (1,)), ((), ())), preferred_element_type=F32)


def kernel(
    nseq,
    nchan,
    gate_hbm,
    key_hbm,
    value_hbm,
    taps_hbm,
    gain_hbm,
    rates_hbm,
    res_hbm,
    weight_hbm,
    out_ref,
    taps_v,
    gain_v,
    rates_v,
    res_v,
    gate_v,
    key_v,
    value_v,
    weight_v,
    perm,
    ext,
    u_ref,
    gs_ref,
    y_ref,
    cin,
    zbuf,
    xbuf,
    tmsg,
    carry,
    edge,
    w_v,
    a_own,
    lead_own,
    states,
    early,
    modes,
    late,
    a_rep,
    lead_rep,
    gathered,
    acc,
    other_acc,
    in_sem,
    z_s,
    z_r,
    x_s,
    x_r,
    early_s,
    early_r,
    late_s,
    late_r,
    own_w,
    sib_s,
    sib_r,
    sum_s,
    sum_r,
    hello_sem,
):
    nx = nseq // NZ
    ny = nchan // 2
    half = ny // 2
    toks = gate_v.shape[1]
    chans = gate_v.shape[0]
    blocks = toks // CHUNKS
    halves = chans // LANES
    seq = lax.axis_index("seq")
    chan = lax.axis_index("chan")
    x, z = seq // NZ, seq % NZ
    y, core = chan // 2, chan % 2
    sibling = chan + 1 - 2 * core

    loads = []
    for n, (src, dst) in enumerate(
        (
            (rates_hbm, rates_v),
            (res_hbm, res_v),
            (taps_hbm, taps_v),
            (key_hbm, key_v),
            (value_hbm, value_v),
            (gate_hbm, gate_v),
            (gain_hbm, gain_v),
        )
    ):
        copy = pltpu.make_async_copy(src, dst, in_sem.at[n])
        copy.start()
        loads.append(copy)

    rows_w = weight_hbm.shape[0]

    def columns(b, of):
        return weight_hbm.at[:, pl.ds(pl.multiple_of((2 * b + of) * chans, chans), chans)]

    def held(b, of):
        return weight_v.at[pl.ds(of * rows_w, rows_w), pl.ds(b * chans, chans)]

    own_weights = [pltpu.make_async_copy(columns(b, core), held(b, 0), own_w.at[b]) for b in range(ny)]
    for copy in own_weights:
        copy.start()

    def along_y(d):
        return ((y + d + ny) % ny) * 2 + core

    def along_z(d):
        return x * NZ + (z + d) % NZ

    barrier = pltpu.get_barrier_semaphore()

    def greet(peer):
        pl.semaphore_signal(barrier, inc=1, device_id=peer, device_id_type=MESH)

    ring = [(dist, 1, dist + 1) for dist in range(half)]
    steps = [(0, 2, 2), (0, 1, 1), (2, 2, 4), (2, 1, 3)] if half == 4 else ring
    near = sorted({way * hop % ny for _, hop, _ in ring + steps for way in (1, -1)})
    for d in near:
        greet((seq, along_y(d)))
    greet((seq, sibling))
    for d in range(1, NZ):
        pl.when(z + d < NZ)(functools.partial(greet, (seq + d, chan)))
    for d in range(1, nx):
        pl.when(x >= d)(functools.partial(greet, (seq - d * NZ, chan)))

    def send(src, dst, ssem, rsem, peer):
        pltpu.make_async_remote_copy(
            src_ref=src,
            dst_ref=dst,
            send_sem=ssem,
            recv_sem=rsem,
            device_id=peer,
            device_id_type=MESH,
        ).start()

    def landing(ref, ssem, rsem):
        return pltpu.make_async_remote_copy(
            src_ref=ref,
            dst_ref=ref,
            send_sem=ssem,
            recv_sem=rsem,
            device_id=(seq, chan),
            device_id_type=MESH,
        )

    def landed(ref, rsem):
        landing(ref, in_sem.at[0], rsem).wait_recv()

    def left(ref, ssem):
        landing(ref, ssem, in_sem.at[0]).wait_send()

    row = lax.broadcasted_iota(jnp.int32, (toks, toks), 0)
    col = lax.broadcasted_iota(jnp.int32, (toks, toks), 1)
    perm[...] = jnp.where(col == (row % CHUNKS) * blocks + row // CHUNKS, 1.0, 0.0).astype(BF16)
    k8 = lax.broadcasted_iota(jnp.int32, (CHUNKS, chans), 0).astype(F32) * float(blocks) + 1.0
    loads[0].wait()
    loads[1].wait()
    r_c = rates_v[...]
    w_c = res_v[...] * jnp.sqrt(r_c)
    w_v[...] = w_c
    modes[y, 0:MODES, :] = r_c[:, 0:LANES]
    modes[y, MODES:, :] = w_c[:, 0:LANES]
    for s in range(MODES):
        a_own[s] = jnp.exp(-jnp.broadcast_to(rates_v[s : s + 1, :], (CHUNKS, chans)))

    def leads(b):
        for s in range(MODES):
            rate = jnp.broadcast_to(modes[b, s : s + 1, :], (CHUNKS, LANES))
            weight = jnp.broadcast_to(modes[b, MODES + s : MODES + s + 1, :], (CHUNKS, LANES))
            a_rep[b, s] = jnp.exp(-rate)
            lead_rep[b, s] = weight * jnp.exp(-rate * k8[:, 0:LANES])

    at_k0 = lax.broadcasted_iota(jnp.int32, (CHUNKS, chans), 0) == 0
    tail = CHUNKS * (blocks - 2)
    loads[2].wait()

    def taps_of(m):
        return [taps_v[3 * m + j : 3 * m + j + 1, :] for j in range(3)]

    def short(m, source):
        laid = nt(perm[...], source[...])
        tap = taps_of(m)
        ext[2 * CHUNKS :, :] = laid
        for n in range(2):
            block = laid[tail + n * CHUNKS : tail + (n + 1) * CHUNKS]
            ext[n * CHUNKS : (n + 1) * CHUNKS, :] = jnp.where(at_k0, 0.0, pltpu.roll(block, 1, 0))
        result = tap[0] * laid
        result = result + tap[1] * ext[CHUNKS : CHUNKS + toks, :]
        result = result + tap[2] * ext[0:toks, :]
        last = laid[toks - 1 : toks]
        prev = laid[toks - 1 - CHUNKS : toks - CHUNKS]
        return result, tap[1] * last + tap[2] * prev, tap[2] * last

    own = zbuf.at[z]
    own[24:MSG, :] = jnp.zeros((MSG - 24, chans), F32)
    loads[3].wait()
    key_short, q0, q1 = short(1, key_v)
    own[16:17, :] = key_short[0:1]
    own[17:18, :] = key_short[CHUNKS : CHUNKS + 1]
    own[20:21, :] = q0
    own[21:22, :] = q1
    loads[4].wait()
    value_short, q0, q1 = short(2, value_v)
    own[18:19, :] = value_short[0:1]
    own[19:20, :] = value_short[CHUNKS : CHUNKS + 1]
    own[22:23, :] = q0
    own[23:24, :] = q1
    u_ref[...] = rounded(key_short * value_short)
    for n in range(2):
        u_ref[n * CHUNKS : n * CHUNKS + 1, :] = jnp.zeros((1, chans), F32)
    loads[5].wait()
    gate_short, q0, q1 = short(0, gate_v)
    own[24:25, :] = q0
    own[25:26, :] = q1

    pl.semaphore_wait(barrier, len(near) + 1 + z + (nx - 1 - x))

    def hello(d):
        pl.semaphore_signal(
            hello_sem.at[d - 1], inc=1, device_id=(seq - d, chan), device_id_type=MESH
        )

    for d in range(1, NZ):
        pl.when(z >= d)(functools.partial(hello, d))

    k3 = lax.broadcasted_iota(jnp.int32, (MODES, CHUNKS, LANES), 1)
    for h in range(halves):
        lanes = slice(h * LANES, (h + 1) * LANES)
        a = a_own[:, :, lanes]

        def scan(i, state):
            u = u_ref[pl.ds(pl.multiple_of(i * CHUNKS, CHUNKS), CHUNKS), lanes]
            return state * a + u[None]

        state = lax.fori_loop(0, blocks, scan, jnp.zeros((MODES, CHUNKS, LANES), F32), unroll=8)
        step = a
        for _ in range(int(math.log2(blocks))):
            step = step * step
        shift = 1
        while shift < CHUNKS:
            moved = jnp.where(k3 >= shift, pltpu.roll(state, shift, 1), 0.0)
            state = state + step * moved
            step = step * step
            shift *= 2
        cin[:, :, lanes] = jnp.where(k3 >= 1, pltpu.roll(state, 1, 1), 0.0)
        for s in range(MODES):
            own[s : s + 1, lanes] = state[s, CHUNKS - 1 : CHUNKS, :]

    def send_state(d):
        send(own, own, z_s.at[d - 1], z_r.at[d - 1], (along_z(d), chan))

    for d in range(1, NZ):
        pl.when(z + d >= NZ)(functools.partial(send_state, d))

    def origin(way, dist):
        return (y + (2 * way - 1) * dist + ny) % ny

    def pass_on(gather, way, src, item):
        routes, parts, side, ssem, rsem = gather
        for at, hop, dist in routes:
            if at == src and (dist < half or way == side(item)):
                for ref, n in parts(origin(way, src), item):
                    sem = (way, dist - 1, n)
                    send(ref, ref, ssem.at[sem], rsem.at[sem], (seq, along_y((1 - 2 * way) * hop)))

    def arrive(gather, dist, items):
        _, parts, side, _, rsem = gather
        for item in items:
            for way in range(2):
                if dist < half or way == side(item):
                    for ref, n in parts(origin(way, dist), item):
                        landed(ref, rsem.at[way, dist - 1, n])
                    pass_on(gather, way, dist, item)

    def all_left(gather, items):
        routes, parts, side, ssem, _ = gather
        for _, _, dist in routes:
            for item in items:
                for way in range(2):
                    if dist < half or way == side(item):
                        for ref, n in parts(y, item):
                            left(ref, ssem.at[way, dist - 1, n])

    GATE, LOCAL = 0, 1

    def early_parts(b, item):
        if item == GATE:
            return (modes.at[b], 2), (early.at[GATE, b], GATE)
        return ((early.at[LOCAL, b], LOCAL),)

    first = (ring, early_parts, lambda item: item, early_s, early_r)

    early[GATE, y] = gate_short[:, 0:LANES].astype(BF16)
    gs_ref[...] = gate_short[:, LANES:]
    for way in range(2):
        pass_on(first, way, 0, GATE)

    loads[6].wait()
    for h in range(halves):
        lanes = slice(h * LANES, (h + 1) * LANES)
        a = a_own[:, :, lanes]
        w = jnp.stack([jnp.broadcast_to(w_v[s : s + 1, lanes], (CHUNKS, LANES)) for s in range(MODES)])
        gain = gain_v[:, lanes]

        def local(i, state):
            both = []
            for n in range(2):
                rows = pl.ds(pl.multiple_of((2 * i + n) * CHUNKS, CHUNKS), CHUNKS)
                u = u_ref[rows, lanes]
                state = state * a + u[None]
                both.append(jnp.sum(state * w, axis=0) + gain * u)
            rows = pl.ds(pl.multiple_of(i * 2 * CHUNKS, 2 * CHUNKS), 2 * CHUNKS)
            if h == 0:
                early[LOCAL, y, rows, :] = jnp.concatenate(both).astype(BF16)
            else:
                y_ref[rows, :] = jnp.concatenate(both)
            return state

        lax.fori_loop(0, blocks // 2, local, cin[:, :, lanes], unroll=2)
        if h == 0:
            for way in range(2):
                pass_on(first, way, 0, LOCAL)
    for s in range(MODES):
        rate = jnp.broadcast_to(rates_v[s : s + 1, :], (CHUNKS, chans))
        lead_own[s] = jnp.broadcast_to(w_v[s : s + 1, :], (CHUNKS, chans)) * jnp.exp(-rate * k8)

    for b in range(ny):
        send(columns(b, 1 - core), held(b, 1), sib_s.at[b], sib_r.at[b], (seq, sibling))

    def gather_first(dists):
        for dist in dists:
            arrive(first, dist, (GATE, LOCAL))
            for way in range(2 if dist < half else 1):
                leads(origin(way, dist))

    gather_first(range(1, min(half, 3)))

    def decay(count):
        return jnp.exp(-r_c * count)

    def edge_tokens(q, msg):
        u0 = rounded((msg[16:17] + q[0:1]) * (msg[18:19] + q[2:3]))
        u1 = rounded((msg[17:18] + q[1:2]) * (msg[19:20] + q[3:4]))
        return u0, u1

    span = float(toks)
    d0, d1, d2 = decay(span), decay(span - 1.0), decay(span - 2.0)
    e0, e1, e2 = decay(NZ * span), decay(NZ * span - 1.0), decay(NZ * span - 2.0)

    def state_of(d):
        landed(zbuf.at[(z + d) % NZ], z_r.at[NZ - d - 1])

    def send_higher(d):
        pl.semaphore_wait(hello_sem.at[d - 1], 1)
        send_state(d)

    for d in range(1, NZ):
        pl.when(z + d < NZ)(functools.partial(send_higher, d))
    for d in range(1, NZ):
        state_of(d)
    msg = zbuf[0]
    cur, q = msg[:MODES], msg[20:26]
    mine, mine_q = jnp.zeros((MODES, chans), F32), jnp.zeros((6, chans), F32)
    for n in range(1, NZ):
        here = z == n
        mine = jnp.where(here, cur, mine)
        mine_q = jnp.where(here, q, mine_q)
        msg = zbuf[n]
        u0, u1 = edge_tokens(q, msg)
        cur = d0 * cur + msg[:MODES] + d1 * u0 + d2 * u1
        q = msg[20:26]
    tmsg[0:MODES, :] = cur
    tmsg[16:20, :] = zbuf[0, 16:20, :]
    tmsg[20:26, :] = q
    tmsg[26:MSG, :] = jnp.zeros((MSG - 26, chans), F32)

    def send_total(d):
        send(tmsg, xbuf.at[x], x_s.at[d - 1], x_r.at[d - 1], (seq + d * NZ, chan))

    for d in range(1, nx):
        pl.when(x + d < nx)(functools.partial(send_total, d))

    gather_first(range(3, half))

    carry[...] = jnp.zeros_like(carry)
    edge[...] = jnp.zeros_like(edge)

    def fold(n):
        landed(xbuf.at[n], x_r.at[x - n - 1])
        msg = xbuf[n]
        u0, u1 = edge_tokens(edge[0:6, :], msg)
        carry[...] = e0 * carry[...] + msg[:MODES] + e1 * u0 + e2 * u1
        edge[0:6, :] = msg[20:26]

    for n in range(nx - 1):
        pl.when(n < x)(functools.partial(fold, n))
    cur, q = carry[...], edge[0:6, :]
    u0, u1 = edge_tokens(q, zbuf[0])
    ahead = z.astype(F32) * span
    inside = mine + decay(ahead) * cur + decay(ahead - 1.0) * u0 + decay(ahead - 2.0) * u1
    at_first = z == 0
    state_in = jnp.where(at_first, cur, inside)
    q = jnp.where(at_first, q, mine_q)
    u0, u1 = edge_tokens(q, own[...])
    back = jnp.exp(r_c)
    gain = gain_v[...]
    states[0:MODES, :] = state_in + back * u0 + back * back * u1
    states[16:17, :] = gain * u0 - jnp.sum(w_c * back, axis=0, keepdims=True) * u1
    states[17:18, :] = gain * u1
    states[18:20, :] = q[4:6]
    states[20:LATE, :] = jnp.zeros((LATE - 20, chans), F32)
    late[y] = states[:, 0:LANES]

    top = lax.broadcasted_iota(jnp.int32, (CHUNKS, LANES), 0) == 0

    def rebuild(a, lead, found, conv_of, gate_of, dst, exact):
        start = jnp.stack(
            [jnp.broadcast_to(found(s), (CHUNKS, LANES)) * lead(s) for s in range(MODES)]
        )
        edges = [found(MODES + n) for n in range(4)]

        def finish(i, state, first_rows=False):
            rows = pl.ds(pl.multiple_of(i * 2 * CHUNKS, 2 * CHUNKS), 2 * CHUNKS)
            conv, gate = conv_of(rows).astype(F32), gate_of(rows).astype(F32)
            both = []
            for n in range(2):
                part = slice(n * CHUNKS, (n + 1) * CHUNKS)
                total, scale = conv[part] + jnp.sum(state, axis=0), gate[part]
                if first_rows:
                    total = total + jnp.where(top, edges[n], 0.0)
                    scale = scale + jnp.where(top, edges[2 + n], 0.0)
                both.append(scale * (rounded(total) if exact else total))
                state = state * a
            dst(rows, jnp.concatenate(both).astype(BF16))
            return state

        lax.fori_loop(1, blocks // 2, finish, finish(0, start, True), unroll=3)

    def store(b, lanes):
        def put(rows, value):
            gathered[b, rows, lanes] = value

        return put

    whole = slice(LANES, 2 * LANES)
    rebuild(
        a_own[:, :, whole],
        lambda s: lead_own[s, :, whole],
        lambda s: states[s : s + 1, whole],
        lambda rows: y_ref[rows, :],
        lambda rows: gs_ref[rows, :],
        store(y, whole),
        True,
    )

    pieces = toks // 2

    def late_parts(b, item):
        if item == 0:
            return ((late.at[b], 0),)
        rows = pl.ds((item - 1) * pieces, pieces)
        return ((gathered.at[b, rows, pl.ds(LANES, LANES)], item),)

    second = (steps, late_parts, lambda item: item // 2, late_s, late_r)
    for item in range(3):
        for way in range(2):
            pass_on(second, way, 0, item)

    def slots(dist):
        return sorted({dist, ny - dist}) if dist else [0]

    def first_half(dist):
        for d in slots(dist):
            b = (y + d) % ny
            rebuild(
                a_rep[b] if d else a_own[:, :, 0:LANES],
                (lambda s: lead_rep[b, s]) if d else (lambda s: lead_own[s, :, 0:LANES]),
                lambda s: late[b, s : s + 1, :],
                lambda rows: early[LOCAL, b, rows, :],
                lambda rows: early[GATE, b, rows, :],
                store(b, slice(0, LANES)),
                False,
            )

    def product(dists, of):
        total = None
        for dist in dists:
            for d in slots(dist):
                b = (y + d) % ny
                cols = pl.ds(pl.multiple_of(b * chans, chans), chans)
                term = nt(weight_v[of * rows_w : (of + 1) * rows_w, cols], gathered[b])
                total = term if total is None else total + term
        return total

    def add(dists):
        for of in range(2):
            acc[of] += product(dists, of)

    for b in range(ny):
        own_weights[b].wait()
        landed(held(b, 1), sib_r.at[b])
    first_half(0)
    for of in range(2):
        acc[of] = product([0], of)
    if half == 4:
        arrive(second, 2, (0,))
        first_half(2)
        arrive(second, 2, (1, 2))
        arrive(second, 1, (0,))
        first_half(1)
        arrive(second, 1, (1, 2))
        add([1, 2])
        arrive(second, 3, (0,))
        first_half(3)
        gather_first([4])
        arrive(second, 4, (0,))
        first_half(4)
        arrive(second, 4, (1, 2))
        arrive(second, 3, (1, 2))
        last = [3, 4]
    else:
        gather_first([half])
        for dist in range(1, half + 1):
            arrive(second, dist, (0, 1, 2))
            first_half(dist)
        last = list(range(1, half + 1))
    acc[1] += product(last, 1)
    send(acc.at[1], other_acc, sum_s.at[0], sum_r.at[0], (seq, sibling))
    acc[0] += product(last, 0)
    landed(other_acc, sum_r.at[0])
    acc[0] += other_acc[...]
    out_ref[...] = jnp.dot(acc[0].astype(BF16), perm[...], preferred_element_type=F32).astype(BF16)

    for d in range(1, NZ):
        left(own, z_s.at[d - 1])
    for d in range(1, nx):
        pl.when(x + d < nx)(functools.partial(left, tmsg, x_s.at[d - 1]))
    all_left(first, (GATE, LOCAL))
    all_left(second, (0, 1, 2))
    for b in range(ny):
        left(columns(b, 1 - core), sib_s.at[b])
    left(acc.at[1], sum_s.at[0])


def body(nseq, nchan, gate, key, value, taps, gain, rates, residues, weight):
    chans, toks = gate.shape
    nx, ny = nseq // NZ, nchan // 2
    vmem = pl.BlockSpec(memory_space=pltpu.VMEM)
    anywhere = pl.BlockSpec(memory_space=pl.ANY)
    dma = pltpu.SemaphoreType.DMA
    return pl.pallas_call(
        functools.partial(kernel, nseq, nchan),
        out_shape=jax.ShapeDtypeStruct((weight.shape[0], toks), BF16),
        in_specs=[anywhere] * 8,
        out_specs=vmem,
        scratch_shapes=[
            pltpu.VMEM(taps.shape, F32),
            pltpu.VMEM((1, chans), F32),
            pltpu.VMEM((MODES, chans), F32),
            pltpu.VMEM((MODES, chans), F32),
            pltpu.VMEM((chans, toks), BF16),
            pltpu.VMEM((chans, toks), BF16),
            pltpu.VMEM((chans, toks), BF16),
            pltpu.VMEM((2 * weight.shape[0], weight.shape[1] // 2), BF16),
            pltpu.VMEM((toks, toks), BF16),
            pltpu.VMEM((toks + 2 * CHUNKS, chans), F32),
            pltpu.VMEM((toks, chans), F32),
            pltpu.VMEM((toks, LANES), F32),
            pltpu.VMEM((toks, LANES), F32),
            pltpu.VMEM((MODES, CHUNKS, chans), F32),
            pltpu.VMEM((NZ, MSG, chans), F32),
            pltpu.VMEM((nx, MSG, chans), F32),
            pltpu.VMEM((MSG, chans), F32),
            pltpu.VMEM((MODES, chans), F32),
            pltpu.VMEM((8, chans), F32),
            pltpu.VMEM((MODES, chans), F32),
            pltpu.VMEM((MODES, CHUNKS, chans), F32),
            pltpu.VMEM((MODES, CHUNKS, chans), F32),
            pltpu.VMEM((LATE, chans), F32),
            pltpu.VMEM((2, ny, toks, LANES), BF16),
            pltpu.VMEM((ny, 2 * MODES, LANES), F32),
            pltpu.VMEM((ny, LATE, LANES), F32),
            pltpu.VMEM((ny, MODES, CHUNKS, LANES), F32),
            pltpu.VMEM((ny, MODES, CHUNKS, LANES), F32),
            pltpu.VMEM((ny, toks, chans), BF16),
            pltpu.VMEM((2, weight.shape[0], toks), F32),
            pltpu.VMEM((weight.shape[0], toks), F32),
            dma((7,)),
            dma((NZ - 1,)),
            dma((NZ - 1,)),
            dma((max(nx - 1, 1),)),
            dma((max(nx - 1, 1),)),
            dma((2, ny // 2, 3)),
            dma((2, ny // 2, 3)),
            dma((2, ny // 2, 3)),
            dma((2, ny // 2, 3)),
            dma((ny,)),
            dma((ny,)),
            dma((ny,)),
            dma((1,)),
            dma((1,)),
            pltpu.SemaphoreType.REGULAR((NZ - 1,)),
        ],
        compiler_params=pltpu.CompilerParams(
            collective_id=0, has_side_effects=True, vmem_limit_bytes=62 * 1024 * 1024
        ),
        name="hyena",
    )(gate, key, value, taps, gain.reshape(1, -1), rates.T, residues.T, weight)


def solution(mesh):
    in_specs = (
        P("chan", "seq"),
        P("chan", "seq"),
        P("chan", "seq"),
        P(None, "chan"),
        P("chan"),
        P("chan", None),
        P("chan", None),
        P("chan", None),
    )
    return jax.shard_map(
        functools.partial(body, mesh.shape["seq"], mesh.shape["chan"]),
        mesh=mesh,
        in_specs=in_specs,
        out_specs=P("chan", "seq"),
        check_vma=False,
    )
```

```python
import functools
import math

import jax
import jax.numpy as jnp
from jax import lax
from jax.experimental import pallas as pl
from jax.experimental.pallas import tpu as pltpu
from jax.sharding import PartitionSpec as P

MESH = pl.DeviceIdType.MESH
F32 = jnp.float32
BF16 = jnp.bfloat16
NZ = 8
MODES = 16
CHUNKS = 8
LANES = 128
MSG = 32
LATE = 24


def rounded(value):
    return value.astype(BF16).astype(F32)


def nt(lhs, rhs):
    return lax.dot_general(lhs, rhs, (((1,), (1,)), ((), ())), preferred_element_type=F32)


def kernel(
    nseq,
    nchan,
    gate_hbm,
    key_hbm,
    value_hbm,
    taps_hbm,
    gain_hbm,
    rates_hbm,
    res_hbm,
    weight_hbm,
    out_ref,
    taps_v,
    gain_v,
    rates_v,
    res_v,
    gate_v,
    key_v,
    value_v,
    weight_v,
    perm,
    ext,
    u_ref,
    gs_ref,
    y_ref,
    cin,
    zbuf,
    xbuf,
    tmsg,
    carry,
    edge,
    w_v,
    a_own,
    lead_own,
    states,
    early,
    modes,
    late,
    a_rep,
    lead_rep,
    gathered,
    acc,
    other_acc,
    in_sem,
    z_s,
    z_r,
    x_s,
    x_r,
    early_s,
    early_r,
    late_s,
    late_r,
    own_w,
    sib_s,
    sib_r,
    sum_s,
    sum_r,
    hello_sem,
):
    nx = nseq // NZ
    ny = nchan // 2
    half = ny // 2
    toks = gate_v.shape[1]
    chans = gate_v.shape[0]
    blocks = toks // CHUNKS
    halves = chans // LANES
    seq = lax.axis_index("seq")
    chan = lax.axis_index("chan")
    x, z = seq // NZ, seq % NZ
    y, core = chan // 2, chan % 2
    sibling = chan + 1 - 2 * core

    loads = []
    for n, (src, dst) in enumerate(
        (
            (rates_hbm, rates_v),
            (res_hbm, res_v),
            (taps_hbm, taps_v),
            (key_hbm, key_v),
            (value_hbm, value_v),
            (gate_hbm, gate_v),
            (gain_hbm, gain_v),
        )
    ):
        copy = pltpu.make_async_copy(src, dst, in_sem.at[n])
        copy.start()
        loads.append(copy)

    rows_w = weight_hbm.shape[0]

    def columns(b, of):
        return weight_hbm.at[:, pl.ds(pl.multiple_of((2 * b + of) * chans, chans), chans)]

    def held(b, of):
        return weight_v.at[pl.ds(of * rows_w, rows_w), pl.ds(b * chans, chans)]

    own_weights = [pltpu.make_async_copy(columns(b, core), held(b, 0), own_w.at[b]) for b in range(ny)]
    for copy in own_weights:
        copy.start()

    def along_y(d):
        return ((y + d + ny) % ny) * 2 + core

    def along_z(d):
        return x * NZ + (z + d) % NZ

    barrier = pltpu.get_barrier_semaphore()

    def greet(peer):
        pl.semaphore_signal(barrier, inc=1, device_id=peer, device_id_type=MESH)

    ring = [(dist, 1, dist + 1) for dist in range(half)]
    steps = [(0, 2, 2), (0, 1, 1), (2, 2, 4), (2, 1, 3)] if half == 4 else ring
    near = sorted({way * hop % ny for _, hop, _ in ring + steps for way in (1, -1)})
    for d in near:
        greet((seq, along_y(d)))
    greet((seq, sibling))
    for d in range(1, NZ):
        pl.when(z + d < NZ)(functools.partial(greet, (seq + d, chan)))
    for d in range(1, nx):
        pl.when(x >= d)(functools.partial(greet, (seq - d * NZ, chan)))

    def send(src, dst, ssem, rsem, peer):
        pltpu.make_async_remote_copy(
            src_ref=src,
            dst_ref=dst,
            send_sem=ssem,
            recv_sem=rsem,
            device_id=peer,
            device_id_type=MESH,
        ).start()

    def landing(ref, ssem, rsem):
        return pltpu.make_async_remote_copy(
            src_ref=ref,
            dst_ref=ref,
            send_sem=ssem,
            recv_sem=rsem,
            device_id=(seq, chan),
            device_id_type=MESH,
        )

    def landed(ref, rsem):
        landing(ref, in_sem.at[0], rsem).wait_recv()

    def left(ref, ssem):
        landing(ref, ssem, in_sem.at[0]).wait_send()

    row = lax.broadcasted_iota(jnp.int32, (toks, toks), 0)
    col = lax.broadcasted_iota(jnp.int32, (toks, toks), 1)
    perm[...] = jnp.where(col == (row % CHUNKS) * blocks + row // CHUNKS, 1.0, 0.0).astype(BF16)
    k8 = lax.broadcasted_iota(jnp.int32, (CHUNKS, chans), 0).astype(F32) * float(blocks) + 1.0
    loads[0].wait()
    loads[1].wait()
    r_c = rates_v[...]
    w_c = res_v[...] * jnp.sqrt(r_c)
    w_v[...] = w_c
    modes[y, 0:MODES, :] = r_c[:, 0:LANES]
    modes[y, MODES:, :] = w_c[:, 0:LANES]
    for s in range(MODES):
        a_own[s] = jnp.exp(-jnp.broadcast_to(rates_v[s : s + 1, :], (CHUNKS, chans)))

    def leads(b):
        for s in range(MODES):
            rate = jnp.broadcast_to(modes[b, s : s + 1, :], (CHUNKS, LANES))
            weight = jnp.broadcast_to(modes[b, MODES + s : MODES + s + 1, :], (CHUNKS, LANES))
            a_rep[b, s] = jnp.exp(-rate)
            lead_rep[b, s] = weight * jnp.exp(-rate * k8[:, 0:LANES])

    at_k0 = lax.broadcasted_iota(jnp.int32, (CHUNKS, chans), 0) == 0
    tail = CHUNKS * (blocks - 2)
    loads[2].wait()

    def taps_of(m):
        return [taps_v[3 * m + j : 3 * m + j + 1, :] for j in range(3)]

    def short(m, source):
        laid = nt(perm[...], source[...])
        tap = taps_of(m)
        ext[2 * CHUNKS :, :] = laid
        for n in range(2):
            block = laid[tail + n * CHUNKS : tail + (n + 1) * CHUNKS]
            ext[n * CHUNKS : (n + 1) * CHUNKS, :] = jnp.where(at_k0, 0.0, pltpu.roll(block, 1, 0))
        result = tap[0] * laid
        result = result + tap[1] * ext[CHUNKS : CHUNKS + toks, :]
        result = result + tap[2] * ext[0:toks, :]
        last = laid[toks - 1 : toks]
        prev = laid[toks - 1 - CHUNKS : toks - CHUNKS]
        return result, tap[1] * last + tap[2] * prev, tap[2] * last

    own = zbuf.at[z]
    own[24:MSG, :] = jnp.zeros((MSG - 24, chans), F32)
    loads[3].wait()
    key_short, q0, q1 = short(1, key_v)
    own[16:17, :] = key_short[0:1]
    own[17:18, :] = key_short[CHUNKS : CHUNKS + 1]
    own[20:21, :] = q0
    own[21:22, :] = q1
    loads[4].wait()
    value_short, q0, q1 = short(2, value_v)
    own[18:19, :] = value_short[0:1]
    own[19:20, :] = value_short[CHUNKS : CHUNKS + 1]
    own[22:23, :] = q0
    own[23:24, :] = q1
    u_ref[...] = rounded(key_short * value_short)
    for n in range(2):
        u_ref[n * CHUNKS : n * CHUNKS + 1, :] = jnp.zeros((1, chans), F32)
    loads[5].wait()
    gate_tap = taps_of(0)
    gate_end = nt(perm[tail:, :], gate_v[...])
    own[24:25, :] = gate_tap[1] * gate_end[15:16] + gate_tap[2] * gate_end[7:8]
    own[25:26, :] = gate_tap[2] * gate_end[15:16]

    pl.semaphore_wait(barrier, len(near) + 1 + z + (nx - 1 - x))

    def hello(d):
        pl.semaphore_signal(
            hello_sem.at[d - 1], inc=1, device_id=(seq - d, chan), device_id_type=MESH
        )

    for d in range(1, NZ):
        pl.when(z >= d)(functools.partial(hello, d))

    k3 = lax.broadcasted_iota(jnp.int32, (MODES, CHUNKS, LANES), 1)
    for h in range(halves):
        lanes = slice(h * LANES, (h + 1) * LANES)
        a = a_own[:, :, lanes]

        def scan(i, state):
            u = u_ref[pl.ds(pl.multiple_of(i * CHUNKS, CHUNKS), CHUNKS), lanes]
            return state * a + u[None]

        state = lax.fori_loop(0, blocks, scan, jnp.zeros((MODES, CHUNKS, LANES), F32), unroll=8)
        step = a
        for _ in range(int(math.log2(blocks))):
            step = step * step
        shift = 1
        while shift < CHUNKS:
            moved = jnp.where(k3 >= shift, pltpu.roll(state, shift, 1), 0.0)
            state = state + step * moved
            step = step * step
            shift *= 2
        cin[:, :, lanes] = jnp.where(k3 >= 1, pltpu.roll(state, 1, 1), 0.0)
        for s in range(MODES):
            own[s : s + 1, lanes] = state[s, CHUNKS - 1 : CHUNKS, :]

    def send_state(d):
        send(own, own, z_s.at[d - 1], z_r.at[d - 1], (along_z(d), chan))

    for d in range(1, NZ):
        pl.when(z + d >= NZ)(functools.partial(send_state, d))

    def origin(way, dist):
        return (y + (2 * way - 1) * dist + ny) % ny

    def pass_on(gather, way, src, item, to=None):
        routes, parts, side, ssem, rsem = gather
        for at, hop, dist in routes:
            if at == src and (dist < half or way == side(item)) and to in (None, dist):
                for ref, n in parts(origin(way, src), item):
                    sem = (way, dist - 1, n)
                    send(ref, ref, ssem.at[sem], rsem.at[sem], (seq, along_y((1 - 2 * way) * hop)))

    def arrive(gather, dist, items):
        _, parts, side, _, rsem = gather
        for item in items:
            for way in range(2):
                if dist < half or way == side(item):
                    for ref, n in parts(origin(way, dist), item):
                        landed(ref, rsem.at[way, dist - 1, n])
                    pass_on(gather, way, dist, item)

    def all_left(gather, items):
        routes, parts, side, ssem, _ = gather
        for _, _, dist in routes:
            for item in items:
                for way in range(2):
                    if dist < half or way == side(item):
                        for ref, n in parts(y, item):
                            left(ref, ssem.at[way, dist - 1, n])

    GATE, LOCAL = 0, 1

    def early_parts(b, item):
        if item == GATE:
            return (modes.at[b], 2), (early.at[GATE, b], GATE)
        return ((early.at[LOCAL, b], LOCAL),)

    first = (ring, early_parts, lambda item: item, early_s, early_r)

    gate_short, _, _ = short(0, gate_v)
    early[GATE, y] = gate_short[:, 0:LANES].astype(BF16)
    gs_ref[...] = gate_short[:, LANES:]
    for way in range(2):
        pass_on(first, way, 0, GATE)

    loads[6].wait()
    for h in range(halves):
        lanes = slice(h * LANES, (h + 1) * LANES)
        a = a_own[:, :, lanes]
        w = jnp.stack([jnp.broadcast_to(w_v[s : s + 1, lanes], (CHUNKS, LANES)) for s in range(MODES)])
        gain = gain_v[:, lanes]

        def local(i, state):
            both = []
            for n in range(2):
                rows = pl.ds(pl.multiple_of((2 * i + n) * CHUNKS, CHUNKS), CHUNKS)
                u = u_ref[rows, lanes]
                state = state * a + u[None]
                both.append(jnp.sum(state * w, axis=0) + gain * u)
            rows = pl.ds(pl.multiple_of(i * 2 * CHUNKS, 2 * CHUNKS), 2 * CHUNKS)
            if h == 0:
                early[LOCAL, y, rows, :] = jnp.concatenate(both).astype(BF16)
            else:
                y_ref[rows, :] = jnp.concatenate(both)
            return state

        lax.fori_loop(0, blocks // 2, local, cin[:, :, lanes], unroll=2)
        if h == 0:
            for way in range(2):
                pass_on(first, way, 0, LOCAL)
    for s in range(MODES):
        rate = jnp.broadcast_to(rates_v[s : s + 1, :], (CHUNKS, chans))
        lead_own[s] = jnp.broadcast_to(w_v[s : s + 1, :], (CHUNKS, chans)) * jnp.exp(-rate * k8)

    for b in range(ny):
        send(columns(b, 1 - core), held(b, 1), sib_s.at[b], sib_r.at[b], (seq, sibling))

    def gather_first(dists):
        for dist in dists:
            arrive(first, dist, (GATE, LOCAL))
            for way in range(2 if dist < half else 1):
                leads(origin(way, dist))

    gather_first(range(1, min(half, 3)))

    def decay(count):
        return jnp.exp(-r_c * count)

    def edge_tokens(q, msg):
        u0 = rounded((msg[16:17] + q[0:1]) * (msg[18:19] + q[2:3]))
        u1 = rounded((msg[17:18] + q[1:2]) * (msg[19:20] + q[3:4]))
        return u0, u1

    top = lax.broadcasted_iota(jnp.int32, (CHUNKS, LANES), 0) == 0

    def rebuild(a, lead, found, conv_of, gate_of, dst, exact, between=None):
        start = jnp.stack(
            [jnp.broadcast_to(found(s), (CHUNKS, LANES)) * lead(s) for s in range(MODES)]
        )
        edges = [found(MODES + n) for n in range(4)]

        def finish(i, state, first_rows=False):
            rows = pl.ds(pl.multiple_of(i * 2 * CHUNKS, 2 * CHUNKS), 2 * CHUNKS)
            conv, gate = conv_of(rows).astype(F32), gate_of(rows).astype(F32)
            both = []
            for n in range(2):
                part = slice(n * CHUNKS, (n + 1) * CHUNKS)
                total, scale = conv[part] + jnp.sum(state, axis=0), gate[part]
                if first_rows:
                    total = total + jnp.where(top, edges[n], 0.0)
                    scale = scale + jnp.where(top, edges[2 + n], 0.0)
                both.append(scale * (rounded(total) if exact else total))
                state = state * a
            dst(rows, jnp.concatenate(both).astype(BF16))
            return state

        state = lax.fori_loop(1, blocks // 4, finish, finish(0, start, True), unroll=True)
        if between is not None:
            between()
        lax.fori_loop(blocks // 4, blocks // 2, finish, state, unroll=True)

    def store(b, lanes):
        def put(rows, value):
            gathered[b, rows, lanes] = value

        return put

    pieces = toks // 2

    def late_parts(b, item):
        if item == 0:
            return ((late.at[b], 0),)
        rows = pl.ds((item - 1) * pieces, pieces)
        return ((gathered.at[b, rows, pl.ds(LANES, LANES)], item),)

    second = (steps, late_parts, lambda item: item // 2, late_s, late_r)

    def launch(state_in, q):
        u0, u1 = edge_tokens(q, own[...])
        back = jnp.exp(r_c)
        gain = gain_v[...]
        states[0:MODES, :] = state_in + back * u0 + back * back * u1
        states[16:17, :] = gain * u0 - jnp.sum(w_c * back, axis=0, keepdims=True) * u1
        states[17:18, :] = gain * u1
        states[18:20, :] = q[4:6]
        states[20:LATE, :] = jnp.zeros((LATE - 20, chans), F32)
        late[y] = states[:, 0:LANES]

        def pass_own(item, to):
            for way in range(2):
                pass_on(second, way, 0, item, to)

        far = steps[0][2]
        pass_own(0, far)
        whole = slice(LANES, 2 * LANES)
        rebuild(
            a_own[:, :, whole],
            lambda s: lead_own[s, :, whole],
            lambda s: states[s : s + 1, whole],
            lambda rows: y_ref[rows, :],
            lambda rows: gs_ref[rows, :],
            store(y, whole),
            True,
            lambda: pass_own(1, far),
        )

        pass_own(2, far)
        if far > 1:
            for item in range(3):
                pass_own(item, 1)

    def launch_first():
        launch(jnp.zeros((MODES, chans), F32), jnp.zeros((6, chans), F32))

    pl.when(seq == 0)(launch_first)

    span = float(toks)
    d0, d1, d2 = decay(span), decay(span - 1.0), decay(span - 2.0)
    e0, e1, e2 = decay(NZ * span), decay(NZ * span - 1.0), decay(NZ * span - 2.0)

    def send_higher(d):
        pl.semaphore_wait(hello_sem.at[d - 1], 1)
        send_state(d)

    for d in range(1, NZ):
        pl.when(z + d < NZ)(functools.partial(send_higher, d))

    def state_of(n):
        landed(zbuf.at[n], z_r.at[(z - n + NZ - 1) % NZ])

    pl.when(z != 0)(functools.partial(state_of, 0))
    msg = zbuf[0]
    cur, q = msg[:MODES], msg[20:26]
    mine, mine_q = jnp.zeros((MODES, chans), F32), jnp.zeros((6, chans), F32)
    for n in range(1, NZ):
        here = z == n
        mine = jnp.where(here, cur, mine)
        mine_q = jnp.where(here, q, mine_q)
        pl.when(z != n)(functools.partial(state_of, n))
        msg = zbuf[n]
        u0, u1 = edge_tokens(q, msg)
        cur = d0 * cur + msg[:MODES] + d1 * u0 + d2 * u1
        q = msg[20:26]
    tmsg[0:MODES, :] = cur
    tmsg[16:20, :] = zbuf[0, 16:20, :]
    tmsg[20:26, :] = q
    tmsg[26:MSG, :] = jnp.zeros((MSG - 26, chans), F32)

    def send_total(d):
        send(tmsg, xbuf.at[x], x_s.at[d - 1], x_r.at[d - 1], (seq + d * NZ, chan))

    for d in range(1, nx):
        pl.when(x + d < nx)(functools.partial(send_total, d))

    gather_first(range(3, half))

    carry[...] = jnp.zeros_like(carry)
    edge[...] = jnp.zeros_like(edge)

    def fold(n):
        landed(xbuf.at[n], x_r.at[x - n - 1])
        msg = xbuf[n]
        u0, u1 = edge_tokens(edge[0:6, :], msg)
        carry[...] = e0 * carry[...] + msg[:MODES] + e1 * u0 + e2 * u1
        edge[0:6, :] = msg[20:26]

    for n in range(nx - 1):
        pl.when(n < x)(functools.partial(fold, n))
    def rest():
        cur, q = carry[...], edge[0:6, :]
        u0, u1 = edge_tokens(q, zbuf[0])
        ahead = z.astype(F32) * span
        inside = mine + decay(ahead) * cur + decay(ahead - 1.0) * u0 + decay(ahead - 2.0) * u1
        at_first = z == 0
        state_in = jnp.where(at_first, cur, inside)
        q = jnp.where(at_first, q, mine_q)
        launch(state_in, q)

    pl.when(seq > 0)(rest)

    def slots(dist):
        return sorted({dist, ny - dist}) if dist else [0]

    def first_half(dist):
        for d in slots(dist):
            b = (y + d) % ny
            rebuild(
                a_rep[b] if d else a_own[:, :, 0:LANES],
                (lambda s: lead_rep[b, s]) if d else (lambda s: lead_own[s, :, 0:LANES]),
                lambda s: late[b, s : s + 1, :],
                lambda rows: early[LOCAL, b, rows, :],
                lambda rows: early[GATE, b, rows, :],
                store(b, slice(0, LANES)),
                False,
            )

    def product(dists, of):
        total = None
        for dist in dists:
            for d in slots(dist):
                b = (y + d) % ny
                cols = pl.ds(pl.multiple_of(b * chans, chans), chans)
                term = nt(weight_v[of * rows_w : (of + 1) * rows_w, cols], gathered[b])
                total = term if total is None else total + term
        return total

    def add(dists):
        for of in range(2):
            acc[of] += product(dists, of)

    for b in range(ny):
        own_weights[b].wait()
        landed(held(b, 1), sib_r.at[b])
    first_half(0)
    for of in range(2):
        acc[of] = product([0], of)
    if half == 4:
        arrive(second, 2, (0, 1, 2))
        first_half(2)
        arrive(second, 1, (0, 1, 2))
        first_half(1)
        add([1, 2])
        arrive(second, 3, (0,))
        first_half(3)
        gather_first([4])
        arrive(second, 4, (0,))
        first_half(4)
        arrive(second, 3, (1, 2))
        add([3])
        arrive(second, 4, (1, 2))
        last = [4]
    else:
        gather_first([half])
        for dist in range(1, half + 1):
            arrive(second, dist, (0, 1, 2))
            first_half(dist)
        last = list(range(1, half + 1))
    acc[1] += product(last, 1)
    send(acc.at[1], other_acc, sum_s.at[0], sum_r.at[0], (seq, sibling))
    acc[0] += product(last, 0)
    landed(other_acc, sum_r.at[0])
    acc[0] += other_acc[...]
    out_ref[...] = jnp.dot(acc[0].astype(BF16), perm[...], preferred_element_type=F32).astype(BF16)

    for d in range(1, NZ):
        left(own, z_s.at[d - 1])
    for d in range(1, nx):
        pl.when(x + d < nx)(functools.partial(left, tmsg, x_s.at[d - 1]))
    all_left(first, (GATE, LOCAL))
    all_left(second, (0, 1, 2))
    for b in range(ny):
        left(columns(b, 1 - core), sib_s.at[b])
    left(acc.at[1], sum_s.at[0])


def body(nseq, nchan, gate, key, value, taps, gain, rates, residues, weight):
    chans, toks = gate.shape
    nx, ny = nseq // NZ, nchan // 2
    vmem = pl.BlockSpec(memory_space=pltpu.VMEM)
    anywhere = pl.BlockSpec(memory_space=pl.ANY)
    dma = pltpu.SemaphoreType.DMA
    return pl.pallas_call(
        functools.partial(kernel, nseq, nchan),
        out_shape=pltpu.VMEM((weight.shape[0], toks), BF16),
        in_specs=[anywhere] * 8,
        out_specs=vmem,
        scratch_shapes=[
            pltpu.VMEM(taps.shape, F32),
            pltpu.VMEM((1, chans), F32),
            pltpu.VMEM((MODES, chans), F32),
            pltpu.VMEM((MODES, chans), F32),
            pltpu.VMEM((chans, toks), BF16),
            pltpu.VMEM((chans, toks), BF16),
            pltpu.VMEM((chans, toks), BF16),
            pltpu.VMEM((2 * weight.shape[0], weight.shape[1] // 2), BF16),
            pltpu.VMEM((toks, toks), BF16),
            pltpu.VMEM((toks + 2 * CHUNKS, chans), F32),
            pltpu.VMEM((toks, chans), F32),
            pltpu.VMEM((toks, LANES), F32),
            pltpu.VMEM((toks, LANES), F32),
            pltpu.VMEM((MODES, CHUNKS, chans), F32),
            pltpu.VMEM((NZ, MSG, chans), F32),
            pltpu.VMEM((nx, MSG, chans), F32),
            pltpu.VMEM((MSG, chans), F32),
            pltpu.VMEM((MODES, chans), F32),
            pltpu.VMEM((8, chans), F32),
            pltpu.VMEM((MODES, chans), F32),
            pltpu.VMEM((MODES, CHUNKS, chans), F32),
            pltpu.VMEM((MODES, CHUNKS, chans), F32),
            pltpu.VMEM((LATE, chans), F32),
            pltpu.VMEM((2, ny, toks, LANES), BF16),
            pltpu.VMEM((ny, 2 * MODES, LANES), F32),
            pltpu.VMEM((ny, LATE, LANES), F32),
            pltpu.VMEM((ny, MODES, CHUNKS, LANES), F32),
            pltpu.VMEM((ny, MODES, CHUNKS, LANES), F32),
            pltpu.VMEM((ny, toks, chans), BF16),
            pltpu.VMEM((2, weight.shape[0], toks), F32),
            pltpu.VMEM((weight.shape[0], toks), F32),
            dma((7,)),
            dma((max(NZ - 1, 1),)),
            dma((max(NZ - 1, 1),)),
            dma((max(nx - 1, 1),)),
            dma((max(nx - 1, 1),)),
            dma((2, ny // 2, 3)),
            dma((2, ny // 2, 3)),
            dma((2, ny // 2, 3)),
            dma((2, ny // 2, 3)),
            dma((ny,)),
            dma((ny,)),
            dma((ny,)),
            dma((1,)),
            dma((1,)),
            pltpu.SemaphoreType.REGULAR((NZ - 1,)),
        ],
        compiler_params=pltpu.CompilerParams(
            collective_id=0, has_side_effects=True, vmem_limit_bytes=60 * 1024 * 1024
        ),
        name="hyena",
    )(gate, key, value, taps, gain.reshape(1, -1), rates.T, residues.T, weight)


def solution(mesh):
    in_specs = (
        P("chan", "seq"),
        P("chan", "seq"),
        P("chan", "seq"),
        P(None, "chan"),
        P("chan"),
        P("chan", None),
        P("chan", None),
        P("chan", None),
    )
    return jax.shard_map(
        functools.partial(body, mesh.shape["seq"], mesh.shape["chan"]),
        mesh=mesh,
        in_specs=in_specs,
        out_specs=P("chan", "seq"),
        check_vma=False,
    )
```

```python
import functools
import math

import jax
import jax.numpy as jnp
from jax import lax
from jax.experimental import pallas as pl
from jax.experimental.pallas import tpu as pltpu
from jax.sharding import PartitionSpec as P

MESH = pl.DeviceIdType.MESH
F32 = jnp.float32
BF16 = jnp.bfloat16
NZ = 8
MODES = 16
CHUNKS = 8
LANES = 128
MSG = 24
LATE = 24


def rounded(value):
    return value.astype(BF16).astype(F32)


def nt(lhs, rhs):
    return lax.dot_general(lhs, rhs, (((1,), (1,)), ((), ())), preferred_element_type=F32)


def kernel(
    nseq,
    nchan,
    gate_hbm,
    key_hbm,
    value_hbm,
    taps_hbm,
    gain_hbm,
    rates_hbm,
    res_hbm,
    weight_hbm,
    out_ref,
    taps_v,
    gain_v,
    rates_v,
    res_v,
    gate_v,
    key_v,
    value_v,
    weight_v,
    perm,
    ext,
    u_ref,
    gs_ref,
    y_ref,
    cin,
    zbuf,
    xbuf,
    tmsg,
    carry,
    last_q,
    gate_edge,
    edge,
    w_v,
    a_own,
    lead_own,
    states,
    early,
    modes,
    late,
    a_rep,
    lead_rep,
    gathered,
    acc,
    other_acc,
    in_sem,
    z_s,
    z_r,
    x_s,
    x_r,
    early_s,
    early_r,
    late_s,
    late_r,
    own_w,
    sib_s,
    sib_r,
    sum_s,
    sum_r,
    edge_s,
    edge_r,
    hello_sem,
):
    nx = nseq // NZ
    ny = nchan // 2
    half = ny // 2
    toks = gate_v.shape[1]
    chans = gate_v.shape[0]
    blocks = toks // CHUNKS
    halves = chans // LANES
    seq = lax.axis_index("seq")
    chan = lax.axis_index("chan")
    x, z = seq // NZ, seq % NZ
    y, core = chan // 2, chan % 2
    sibling = chan + 1 - 2 * core

    loads = []
    for n, (src, dst) in enumerate(
        (
            (rates_hbm, rates_v),
            (res_hbm, res_v),
            (taps_hbm, taps_v),
            (key_hbm, key_v),
            (value_hbm, value_v),
            (gate_hbm, gate_v),
            (gain_hbm, gain_v),
        )
    ):
        copy = pltpu.make_async_copy(src, dst, in_sem.at[n])
        copy.start()
        loads.append(copy)

    rows_w = weight_hbm.shape[0]

    def columns(b, of):
        return weight_hbm.at[:, pl.ds(pl.multiple_of((2 * b + of) * chans, chans), chans)]

    def held(b, of):
        return weight_v.at[pl.ds(of * rows_w, rows_w), pl.ds(b * chans, chans)]

    own_weights = [pltpu.make_async_copy(columns(b, core), held(b, 0), own_w.at[b]) for b in range(ny)]
    def along_y(d):
        return ((y + d + ny) % ny) * 2 + core

    def along_z(d):
        return x * NZ + (z + d) % NZ

    barrier = pltpu.get_barrier_semaphore()

    def greet(peer):
        pl.semaphore_signal(barrier, inc=1, device_id=peer, device_id_type=MESH)

    ring = [(dist, 1, dist + 1) for dist in range(half)]
    steps = [(0, 2, 2), (0, 1, 1), (2, 2, 4), (2, 1, 3)] if half == 4 else ring
    near = sorted({way * hop % ny for _, hop, _ in ring + steps for way in (1, -1)})
    for d in near:
        greet((seq, along_y(d)))
    greet((seq, sibling))
    pl.when((z == 0) & (x > 0))(functools.partial(greet, (seq - 1, chan)))
    for d in range(1, NZ):
        pl.when(z + d < NZ)(functools.partial(greet, (seq + d, chan)))
    for d in range(1, nx):
        pl.when(x >= d)(functools.partial(greet, (seq - d * NZ, chan)))

    def send(src, dst, ssem, rsem, peer):
        pltpu.make_async_remote_copy(
            src_ref=src,
            dst_ref=dst,
            send_sem=ssem,
            recv_sem=rsem,
            device_id=peer,
            device_id_type=MESH,
        ).start()

    def landing(ref, ssem, rsem):
        return pltpu.make_async_remote_copy(
            src_ref=ref,
            dst_ref=ref,
            send_sem=ssem,
            recv_sem=rsem,
            device_id=(seq, chan),
            device_id_type=MESH,
        )

    def landed(ref, rsem):
        landing(ref, in_sem.at[0], rsem).wait_recv()

    def left(ref, ssem):
        landing(ref, ssem, in_sem.at[0]).wait_send()

    row = lax.broadcasted_iota(jnp.int32, (toks, toks), 0)
    col = lax.broadcasted_iota(jnp.int32, (toks, toks), 1)
    perm[...] = jnp.where(col == (row % CHUNKS) * blocks + row // CHUNKS, 1.0, 0.0).astype(BF16)
    k8 = lax.broadcasted_iota(jnp.int32, (CHUNKS, chans), 0).astype(F32) * float(blocks) + 1.0
    loads[0].wait()
    loads[1].wait()
    r_c = rates_v[...]
    w_c = res_v[...] * jnp.sqrt(r_c)
    w_v[...] = w_c
    modes[y, 0:MODES, :] = r_c[:, 0:LANES]
    modes[y, MODES:, :] = w_c[:, 0:LANES]
    for s in range(MODES):
        a_own[s] = jnp.exp(-jnp.broadcast_to(rates_v[s : s + 1, :], (CHUNKS, chans)))

    def leads(b):
        for s in range(MODES):
            rate = jnp.broadcast_to(modes[b, s : s + 1, :], (CHUNKS, LANES))
            weight = jnp.broadcast_to(modes[b, MODES + s : MODES + s + 1, :], (CHUNKS, LANES))
            a_rep[b, s] = jnp.exp(-rate)
            lead_rep[b, s] = weight * jnp.exp(-rate * k8[:, 0:LANES])

    at_k0 = lax.broadcasted_iota(jnp.int32, (CHUNKS, chans), 0) == 0
    tail = CHUNKS * (blocks - 2)
    loads[2].wait()

    def taps_of(m):
        return [taps_v[3 * m + j : 3 * m + j + 1, :] for j in range(3)]

    def short(m, source):
        laid = nt(perm[...], source[...])
        tap = taps_of(m)
        ext[2 * CHUNKS :, :] = laid
        for n in range(2):
            block = laid[tail + n * CHUNKS : tail + (n + 1) * CHUNKS]
            ext[n * CHUNKS : (n + 1) * CHUNKS, :] = jnp.where(at_k0, 0.0, pltpu.roll(block, 1, 0))
        result = tap[0] * laid
        result = result + tap[1] * ext[CHUNKS : CHUNKS + toks, :]
        result = result + tap[2] * ext[0:toks, :]
        last = laid[toks - 1 : toks]
        prev = laid[toks - 1 - CHUNKS : toks - CHUNKS]
        return result, tap[1] * last + tap[2] * prev, tap[2] * last

    own = zbuf.at[z]
    loads[3].wait()
    key_short, q0, q1 = short(1, key_v)
    own[16:17, :] = key_short[0:1]
    own[17:18, :] = key_short[CHUNKS : CHUNKS + 1]
    own[20:21, :] = q0
    own[21:22, :] = q1
    loads[4].wait()
    value_short, q0, q1 = short(2, value_v)
    own[18:19, :] = value_short[0:1]
    own[19:20, :] = value_short[CHUNKS : CHUNKS + 1]
    own[22:23, :] = q0
    own[23:24, :] = q1
    u_ref[...] = rounded(key_short * value_short)
    for n in range(2):
        u_ref[n * CHUNKS : n * CHUNKS + 1, :] = jnp.zeros((1, chans), F32)

    follows = jnp.where((z == NZ - 1) & (x < nx - 1), 1, 0)
    pl.semaphore_wait(barrier, len(near) + 1 + z + (nx - 1 - x) + follows)

    k3 = lax.broadcasted_iota(jnp.int32, (MODES, CHUNKS, LANES), 1)
    for h in range(halves):
        lanes = slice(h * LANES, (h + 1) * LANES)
        a = a_own[:, :, lanes]

        def scan(i, state):
            u = u_ref[pl.ds(pl.multiple_of(i * CHUNKS, CHUNKS), CHUNKS), lanes]
            return state * a + u[None]

        state = lax.fori_loop(0, blocks, scan, jnp.zeros((MODES, CHUNKS, LANES), F32), unroll=8)
        step = a
        for _ in range(int(math.log2(blocks))):
            step = step * step
        shift = 1
        while shift < CHUNKS:
            moved = jnp.where(k3 >= shift, pltpu.roll(state, shift, 1), 0.0)
            state = state + step * moved
            step = step * step
            shift *= 2
        cin[:, :, lanes] = jnp.where(k3 >= 1, pltpu.roll(state, 1, 1), 0.0)
        for s in range(MODES):
            own[s : s + 1, lanes] = state[s, CHUNKS - 1 : CHUNKS, :]

    def send_state(d):
        send(own, own, z_s.at[d - 1], z_r.at[d - 1], (along_z(d), chan))

    def send_edge():
        send(gate_edge, edge, edge_s.at[0], edge_r.at[0], (seq + 1, chan))

    for d in range(1, NZ):
        pl.when(z + d >= NZ)(functools.partial(send_state, d))

    def hello(d):
        pl.semaphore_signal(
            hello_sem.at[d - 1], inc=1, device_id=(seq - d, chan), device_id_type=MESH
        )

    for d in range(1, NZ):
        pl.when(z >= d)(functools.partial(hello, d))

    for copy in own_weights:
        copy.start()

    def origin(way, dist):
        return (y + (2 * way - 1) * dist + ny) % ny

    def pass_on(gather, way, src, item, to=None):
        routes, parts, side, ssem, rsem = gather
        for at, hop, dist in routes:
            if at == src and (dist < half or way == side(item)) and to in (None, dist):
                for ref, n in parts(origin(way, src), item):
                    sem = (way, dist - 1, n)
                    send(ref, ref, ssem.at[sem], rsem.at[sem], (seq, along_y((1 - 2 * way) * hop)))

    def arrive(gather, dist, items):
        _, parts, side, _, rsem = gather
        for item in items:
            for way in range(2):
                if dist < half or way == side(item):
                    for ref, n in parts(origin(way, dist), item):
                        landed(ref, rsem.at[way, dist - 1, n])
                    pass_on(gather, way, dist, item)

    def all_left(gather, items):
        routes, parts, side, ssem, _ = gather
        for _, _, dist in routes:
            for item in items:
                for way in range(2):
                    if dist < half or way == side(item):
                        for ref, n in parts(y, item):
                            left(ref, ssem.at[way, dist - 1, n])

    GATE, LOCAL = 0, 1

    def early_parts(b, item):
        if item == GATE:
            return (modes.at[b], 2), (early.at[GATE, b], GATE)
        return ((early.at[LOCAL, b], LOCAL),)

    first = (ring, early_parts, lambda item: item, early_s, early_r)

    loads[5].wait()
    gate_short, q0, q1 = short(0, gate_v)
    gate_edge[0:1, :] = q0
    gate_edge[1:2, :] = q1
    gate_edge[2:8, :] = jnp.zeros((6, chans), F32)
    pl.when((z == NZ - 1) & (x < nx - 1))(send_edge)
    early[GATE, y] = gate_short[:, 0:LANES].astype(BF16)
    gs_ref[...] = gate_short[:, LANES:]
    for way in range(2):
        pass_on(first, way, 0, GATE)

    loads[6].wait()
    for h in range(halves):
        lanes = slice(h * LANES, (h + 1) * LANES)
        a = a_own[:, :, lanes]
        w = jnp.stack([jnp.broadcast_to(w_v[s : s + 1, lanes], (CHUNKS, LANES)) for s in range(MODES)])
        gain = gain_v[:, lanes]

        def local(i, state):
            both = []
            for n in range(2):
                rows = pl.ds(pl.multiple_of((2 * i + n) * CHUNKS, CHUNKS), CHUNKS)
                u = u_ref[rows, lanes]
                state = state * a + u[None]
                both.append(jnp.sum(state * w, axis=0) + gain * u)
            rows = pl.ds(pl.multiple_of(i * 2 * CHUNKS, 2 * CHUNKS), 2 * CHUNKS)
            if h == 0:
                early[LOCAL, y, rows, :] = jnp.concatenate(both).astype(BF16)
            else:
                y_ref[rows, :] = jnp.concatenate(both)
            return state

        lax.fori_loop(0, blocks // 2, local, cin[:, :, lanes], unroll=2)
        if h == 0:
            for way in range(2):
                pass_on(first, way, 0, LOCAL)
    for s in range(MODES):
        rate = jnp.broadcast_to(rates_v[s : s + 1, :], (CHUNKS, chans))
        lead_own[s] = jnp.broadcast_to(w_v[s : s + 1, :], (CHUNKS, chans)) * jnp.exp(-rate * k8)

    for b in range(ny):
        send(columns(b, 1 - core), held(b, 1), sib_s.at[b], sib_r.at[b], (seq, sibling))

    def gather_first(dists):
        for dist in dists:
            arrive(first, dist, (GATE, LOCAL))
            for way in range(2 if dist < half else 1):
                leads(origin(way, dist))

    gather_first(range(1, min(half, 3)))

    def decay(count):
        return jnp.exp(-r_c * count)

    def edge_tokens(q, msg):
        u0 = rounded((msg[16:17] + q[0:1]) * (msg[18:19] + q[2:3]))
        u1 = rounded((msg[17:18] + q[1:2]) * (msg[19:20] + q[3:4]))
        return u0, u1

    top = lax.broadcasted_iota(jnp.int32, (CHUNKS, LANES), 0) == 0

    def rebuild(a, lead, found, conv_of, gate_of, dst, exact, between=None):
        start = jnp.stack(
            [jnp.broadcast_to(found(s), (CHUNKS, LANES)) * lead(s) for s in range(MODES)]
        )
        edges = [found(MODES + n) for n in range(4)]

        def finish(i, state, first_rows=False):
            rows = pl.ds(pl.multiple_of(i * 2 * CHUNKS, 2 * CHUNKS), 2 * CHUNKS)
            conv, gate = conv_of(rows).astype(F32), gate_of(rows).astype(F32)
            both = []
            for n in range(2):
                part = slice(n * CHUNKS, (n + 1) * CHUNKS)
                total, scale = conv[part] + jnp.sum(state, axis=0), gate[part]
                if first_rows:
                    total = total + jnp.where(top, edges[n], 0.0)
                    scale = scale + jnp.where(top, edges[2 + n], 0.0)
                both.append(scale * (rounded(total) if exact else total))
                state = state * a
            dst(rows, jnp.concatenate(both).astype(BF16))
            return state

        state = lax.fori_loop(1, blocks // 4, finish, finish(0, start, True), unroll=True)
        if between is not None:
            between()
        lax.fori_loop(blocks // 4, blocks // 2, finish, state, unroll=True)

    def store(b, lanes):
        def put(rows, value):
            gathered[b, rows, lanes] = value

        return put

    pieces = toks // 2

    def late_parts(b, item):
        if item == 0:
            return ((late.at[b], 0),)
        rows = pl.ds((item - 1) * pieces, pieces)
        return ((gathered.at[b, rows, pl.ds(LANES, LANES)], item),)

    second = (steps, late_parts, lambda item: item // 2, late_s, late_r)

    back = jnp.exp(r_c)
    early_token = jnp.sum(w_c * back, axis=0, keepdims=True)

    def launch(state_in, q, halo):
        u0, u1 = edge_tokens(q, own[...])
        gain = gain_v[...]
        states[0:MODES, :] = state_in + back * u0 + back * back * u1
        states[16:17, :] = gain * u0 - early_token * u1
        states[17:18, :] = gain * u1
        states[18:20, :] = halo
        states[20:LATE, :] = jnp.zeros((LATE - 20, chans), F32)
        late[y] = states[:, 0:LANES]

        def pass_own(item, to):
            for way in range(2):
                pass_on(second, way, 0, item, to)

        far = steps[0][2]
        pass_own(0, far)
        whole = slice(LANES, 2 * LANES)
        rebuild(
            a_own[:, :, whole],
            lambda s: lead_own[s, :, whole],
            lambda s: states[s : s + 1, whole],
            lambda rows: y_ref[rows, :],
            lambda rows: gs_ref[rows, :],
            store(y, whole),
            True,
            lambda: pass_own(1, far),
        )

        pass_own(2, far)
        if far > 1:
            for item in range(3):
                pass_own(item, 1)

    def launch_first():
        launch(jnp.zeros((MODES, chans), F32), jnp.zeros((4, chans), F32), jnp.zeros((2, chans), F32))

    pl.when(seq == 0)(launch_first)

    span = float(toks)
    d0, d1, d2 = decay(span), decay(span - 1.0), decay(span - 2.0)
    ahead = z.astype(F32) * span
    a0, a1, a2 = decay(ahead), decay(ahead - 1.0), decay(ahead - 2.0)
    e0, e1, e2 = decay(NZ * span), decay(NZ * span - 1.0), decay(NZ * span - 2.0)

    def send_higher(d):
        pl.semaphore_wait(hello_sem.at[d - 1], 1)
        send_state(d)
        if d == 1:
            send_edge()

    for d in range(1, NZ):
        pl.when(z + d < NZ)(functools.partial(send_higher, d))

    def state_of(n):
        landed(zbuf.at[n], z_r.at[(z - n + NZ - 1) % NZ])

    pl.when(z != 0)(functools.partial(state_of, 0))
    msg = zbuf[0]
    cur, q = msg[:MODES], msg[20:24]
    mine, mine_q = jnp.zeros((MODES, chans), F32), jnp.zeros((4, chans), F32)
    for n in range(1, NZ):
        here = z == n
        mine = jnp.where(here, cur, mine)
        mine_q = jnp.where(here, q, mine_q)
        pl.when(z != n)(functools.partial(state_of, n))
        msg = zbuf[n]
        u0, u1 = edge_tokens(q, msg)
        cur = d0 * cur + msg[:MODES] + d1 * u0 + d2 * u1
        q = msg[20:24]
    tmsg[0:MODES, :] = cur
    tmsg[16:20, :] = zbuf[0, 16:20, :]
    tmsg[20:24, :] = q

    def send_total(d):
        send(tmsg, xbuf.at[x], x_s.at[d - 1], x_r.at[d - 1], (seq + d * NZ, chan))

    for d in range(1, nx):
        pl.when(x + d < nx)(functools.partial(send_total, d))

    gather_first(range(3, half))

    carry[...] = jnp.zeros_like(carry)
    last_q[...] = jnp.zeros_like(last_q)

    def fold(n):
        landed(xbuf.at[n], x_r.at[x - n - 1])
        msg = xbuf[n]
        u0, u1 = edge_tokens(last_q[0:4, :], msg)
        carry[...] = e0 * carry[...] + msg[:MODES] + e1 * u0 + e2 * u1
        last_q[0:4, :] = msg[20:24]

    for n in range(nx - 1):
        pl.when(n < x)(functools.partial(fold, n))
    def rest():
        cur, q = carry[...], last_q[0:4, :]
        u0, u1 = edge_tokens(q, zbuf[0])
        inside = mine + a0 * cur + a1 * u0 + a2 * u1
        at_first = z == 0
        state_in = jnp.where(at_first, cur, inside)
        q = jnp.where(at_first, q, mine_q)
        landed(edge, edge_r.at[0])
        launch(state_in, q, edge[0:2, :])

    pl.when(seq > 0)(rest)

    def slots(dist):
        return sorted({dist, ny - dist}) if dist else [0]

    def first_half(dist):
        for d in slots(dist):
            b = (y + d) % ny
            rebuild(
                a_rep[b] if d else a_own[:, :, 0:LANES],
                (lambda s: lead_rep[b, s]) if d else (lambda s: lead_own[s, :, 0:LANES]),
                lambda s: late[b, s : s + 1, :],
                lambda rows: early[LOCAL, b, rows, :],
                lambda rows: early[GATE, b, rows, :],
                store(b, slice(0, LANES)),
                False,
            )

    def product(dists, of):
        total = None
        for dist in dists:
            for d in slots(dist):
                b = (y + d) % ny
                cols = pl.ds(pl.multiple_of(b * chans, chans), chans)
                term = nt(weight_v[of * rows_w : (of + 1) * rows_w, cols], gathered[b])
                total = term if total is None else total + term
        return total

    def add(dists):
        for of in range(2):
            acc[of] += product(dists, of)

    for b in range(ny):
        own_weights[b].wait()
        landed(held(b, 1), sib_r.at[b])
    first_half(0)
    for of in range(2):
        acc[of] = product([0], of)
    if half == 4:
        arrive(second, 2, (0, 1, 2))
        first_half(2)
        arrive(second, 1, (0, 1, 2))
        first_half(1)
        add([1, 2])
        arrive(second, 3, (0,))
        first_half(3)
        gather_first([4])
        arrive(second, 4, (0,))
        first_half(4)
        arrive(second, 3, (1, 2))
        add([3])
        arrive(second, 4, (1, 2))
        last = [4]
    else:
        gather_first([half])
        for dist in range(1, half + 1):
            arrive(second, dist, (0, 1, 2))
            first_half(dist)
        last = list(range(1, half + 1))
    acc[1] += product(last, 1)
    send(acc.at[1], other_acc, sum_s.at[0], sum_r.at[0], (seq, sibling))
    acc[0] += product(last, 0)
    landed(other_acc, sum_r.at[0])
    acc[0] += other_acc[...]
    out_ref[...] = jnp.dot(acc[0].astype(BF16), perm[...], preferred_element_type=F32).astype(BF16)

    for d in range(1, NZ):
        left(own, z_s.at[d - 1])
    for d in range(1, nx):
        pl.when(x + d < nx)(functools.partial(left, tmsg, x_s.at[d - 1]))
    pl.when(seq < nseq - 1)(functools.partial(left, gate_edge, edge_s.at[0]))
    all_left(first, (GATE, LOCAL))
    all_left(second, (0, 1, 2))
    for b in range(ny):
        left(columns(b, 1 - core), sib_s.at[b])
    left(acc.at[1], sum_s.at[0])


def body(nseq, nchan, gate, key, value, taps, gain, rates, residues, weight):
    chans, toks = gate.shape
    nx, ny = nseq // NZ, nchan // 2
    vmem = pl.BlockSpec(memory_space=pltpu.VMEM)
    anywhere = pl.BlockSpec(memory_space=pl.ANY)
    dma = pltpu.SemaphoreType.DMA
    return pl.pallas_call(
        functools.partial(kernel, nseq, nchan),
        out_shape=pltpu.VMEM((weight.shape[0], toks), BF16),
        in_specs=[anywhere] * 8,
        out_specs=vmem,
        scratch_shapes=[
            pltpu.VMEM(taps.shape, F32),
            pltpu.VMEM((1, chans), F32),
            pltpu.VMEM((MODES, chans), F32),
            pltpu.VMEM((MODES, chans), F32),
            pltpu.VMEM((chans, toks), BF16),
            pltpu.VMEM((chans, toks), BF16),
            pltpu.VMEM((chans, toks), BF16),
            pltpu.VMEM((2 * weight.shape[0], weight.shape[1] // 2), BF16),
            pltpu.VMEM((toks, toks), BF16),
            pltpu.VMEM((toks + 2 * CHUNKS, chans), F32),
            pltpu.VMEM((toks, chans), F32),
            pltpu.VMEM((toks, LANES), F32),
            pltpu.VMEM((toks, LANES), F32),
            pltpu.VMEM((MODES, CHUNKS, chans), F32),
            pltpu.VMEM((NZ, MSG, chans), F32),
            pltpu.VMEM((nx, MSG, chans), F32),
            pltpu.VMEM((MSG, chans), F32),
            pltpu.VMEM((MODES, chans), F32),
            pltpu.VMEM((8, chans), F32),
            pltpu.VMEM((8, chans), F32),
            pltpu.VMEM((8, chans), F32),
            pltpu.VMEM((MODES, chans), F32),
            pltpu.VMEM((MODES, CHUNKS, chans), F32),
            pltpu.VMEM((MODES, CHUNKS, chans), F32),
            pltpu.VMEM((LATE, chans), F32),
            pltpu.VMEM((2, ny, toks, LANES), BF16),
            pltpu.VMEM((ny, 2 * MODES, LANES), F32),
            pltpu.VMEM((ny, LATE, LANES), F32),
            pltpu.VMEM((ny, MODES, CHUNKS, LANES), F32),
            pltpu.VMEM((ny, MODES, CHUNKS, LANES), F32),
            pltpu.VMEM((ny, toks, chans), BF16),
            pltpu.VMEM((2, weight.shape[0], toks), F32),
            pltpu.VMEM((weight.shape[0], toks), F32),
            dma((7,)),
            dma((max(NZ - 1, 1),)),
            dma((max(NZ - 1, 1),)),
            dma((max(nx - 1, 1),)),
            dma((max(nx - 1, 1),)),
            dma((2, ny // 2, 3)),
            dma((2, ny // 2, 3)),
            dma((2, ny // 2, 3)),
            dma((2, ny // 2, 3)),
            dma((ny,)),
            dma((ny,)),
            dma((ny,)),
            dma((1,)),
            dma((1,)),
            dma((1,)),
            dma((1,)),
            pltpu.SemaphoreType.REGULAR((max(NZ - 1, 1),)),
        ],
        compiler_params=pltpu.CompilerParams(
            collective_id=0, has_side_effects=True, vmem_limit_bytes=60 * 1024 * 1024
        ),
        name="hyena",
    )(gate, key, value, taps, gain.reshape(1, -1), rates.T, residues.T, weight)


def solution(mesh):
    in_specs = (
        P("chan", "seq"),
        P("chan", "seq"),
        P("chan", "seq"),
        P(None, "chan"),
        P("chan"),
        P("chan", None),
        P("chan", None),
        P("chan", None),
    )
    return jax.shard_map(
        functools.partial(body, mesh.shape["seq"], mesh.shape["chan"]),
        mesh=mesh,
        in_specs=in_specs,
        out_specs=P("chan", "seq"),
        check_vma=False,
    )
```

```python
import functools
import math

import jax
import jax.numpy as jnp
from jax import lax
from jax.experimental import pallas as pl
from jax.experimental.pallas import tpu as pltpu
from jax.sharding import PartitionSpec as P

MESH = pl.DeviceIdType.MESH
F32 = jnp.float32
BF16 = jnp.bfloat16
NZ = 8
MODES = 16
CHUNKS = 8
LANES = 128
MSG = 24
LATE = 24


def rounded(value):
    return value.astype(BF16).astype(F32)


def nt(lhs, rhs):
    return lax.dot_general(lhs, rhs, (((1,), (1,)), ((), ())), preferred_element_type=F32)


def kernel(
    nseq,
    nchan,
    gate_hbm,
    key_hbm,
    value_hbm,
    taps_hbm,
    gain_hbm,
    rates_hbm,
    res_hbm,
    weight_hbm,
    out_ref,
    taps_v,
    gain_v,
    rates_v,
    res_v,
    gate_v,
    key_v,
    value_v,
    weight_v,
    perm,
    ext,
    u_ref,
    gs_ref,
    y_ref,
    cin,
    zbuf,
    xbuf,
    tmsg,
    carry,
    last_q,
    gate_edge,
    edge,
    w_v,
    a_own,
    lead_own,
    states,
    early,
    modes,
    late,
    a_rep,
    lead_rep,
    gathered,
    acc,
    other_acc,
    in_sem,
    z_s,
    z_r,
    x_s,
    x_r,
    early_s,
    early_r,
    late_s,
    late_r,
    own_w,
    sib_s,
    sib_r,
    sum_s,
    sum_r,
    edge_s,
    edge_r,
    hello_sem,
):
    nx = nseq // NZ
    ny = nchan // 2
    half = ny // 2
    toks = gate_v.shape[1]
    chans = gate_v.shape[0]
    blocks = toks // CHUNKS
    halves = chans // LANES
    seq = lax.axis_index("seq")
    chan = lax.axis_index("chan")
    x, z = seq // NZ, seq % NZ
    y, core = chan // 2, chan % 2
    sibling = chan + 1 - 2 * core

    loads = []
    for n, (src, dst) in enumerate(
        (
            (rates_hbm, rates_v),
            (res_hbm, res_v),
            (taps_hbm, taps_v),
            (key_hbm, key_v),
            (value_hbm, value_v),
            (gate_hbm, gate_v),
            (gain_hbm, gain_v),
        )
    ):
        copy = pltpu.make_async_copy(src, dst, in_sem.at[n])
        copy.start()
        loads.append(copy)

    rows_w = weight_hbm.shape[0]

    def columns(b, of):
        return weight_hbm.at[:, pl.ds(pl.multiple_of((2 * b + of) * chans, chans), chans)]

    def held(b, of):
        return weight_v.at[pl.ds(of * rows_w, rows_w), pl.ds(b * chans, chans)]

    own_weights = [pltpu.make_async_copy(columns(b, core), held(b, 0), own_w.at[b]) for b in range(ny)]
    def along_y(d):
        return ((y + d + ny) % ny) * 2 + core

    def along_z(d):
        return x * NZ + (z + d) % NZ

    barrier = pltpu.get_barrier_semaphore()

    def greet(peer):
        pl.semaphore_signal(barrier, inc=1, device_id=peer, device_id_type=MESH)

    ring = [(dist, 1, dist + 1) for dist in range(half)]
    steps = [(0, 2, 2), (0, 1, 1), (2, 2, 4), (2, 1, 3)] if half == 4 else ring
    near = sorted({way * hop % ny for _, hop, _ in ring + steps for way in (1, -1)})
    for d in near:
        greet((seq, along_y(d)))
    greet((seq, sibling))
    pl.when((z == 0) & (x > 0))(functools.partial(greet, (seq - 1, chan)))
    for d in range(1, NZ):
        pl.when(z + d < NZ)(functools.partial(greet, (seq + d, chan)))
    for d in range(1, nx):
        pl.when(x >= d)(functools.partial(greet, (seq - d * NZ, chan)))

    def send(src, dst, ssem, rsem, peer):
        pltpu.make_async_remote_copy(
            src_ref=src,
            dst_ref=dst,
            send_sem=ssem,
            recv_sem=rsem,
            device_id=peer,
            device_id_type=MESH,
        ).start()

    def landing(ref, ssem, rsem):
        return pltpu.make_async_remote_copy(
            src_ref=ref,
            dst_ref=ref,
            send_sem=ssem,
            recv_sem=rsem,
            device_id=(seq, chan),
            device_id_type=MESH,
        )

    def landed(ref, rsem):
        landing(ref, in_sem.at[0], rsem).wait_recv()

    def left(ref, ssem):
        landing(ref, ssem, in_sem.at[0]).wait_send()

    row = lax.broadcasted_iota(jnp.int32, (toks, toks), 0)
    col = lax.broadcasted_iota(jnp.int32, (toks, toks), 1)
    perm[...] = jnp.where(col == (row % CHUNKS) * blocks + row // CHUNKS, 1.0, 0.0).astype(BF16)
    k8 = lax.broadcasted_iota(jnp.int32, (CHUNKS, chans), 0).astype(F32) * float(blocks) + 1.0
    loads[0].wait()
    loads[1].wait()
    r_c = rates_v[...]
    w_c = res_v[...] * jnp.sqrt(r_c)
    w_v[...] = w_c
    modes[y, 0:MODES, :] = r_c[:, 0:LANES]
    modes[y, MODES:, :] = w_c[:, 0:LANES]
    for s in range(MODES):
        a_own[s] = jnp.exp(-jnp.broadcast_to(rates_v[s : s + 1, :], (CHUNKS, chans)))

    def leads(b):
        for s in range(MODES):
            rate = jnp.broadcast_to(modes[b, s : s + 1, :], (CHUNKS, LANES))
            weight = jnp.broadcast_to(modes[b, MODES + s : MODES + s + 1, :], (CHUNKS, LANES))
            a_rep[b, s] = jnp.exp(-rate)
            lead_rep[b, s] = weight * jnp.exp(-rate * k8[:, 0:LANES])

    at_k0 = lax.broadcasted_iota(jnp.int32, (CHUNKS, chans), 0) == 0
    tail = CHUNKS * (blocks - 2)
    loads[2].wait()

    def taps_of(m):
        return [taps_v[3 * m + j : 3 * m + j + 1, :] for j in range(3)]

    def short(m, source):
        laid = nt(perm[...], source[...])
        tap = taps_of(m)
        ext[2 * CHUNKS :, :] = laid
        for n in range(2):
            block = laid[tail + n * CHUNKS : tail + (n + 1) * CHUNKS]
            ext[n * CHUNKS : (n + 1) * CHUNKS, :] = jnp.where(at_k0, 0.0, pltpu.roll(block, 1, 0))
        result = tap[0] * laid
        result = result + tap[1] * ext[CHUNKS : CHUNKS + toks, :]
        result = result + tap[2] * ext[0:toks, :]
        last = laid[toks - 1 : toks]
        prev = laid[toks - 1 - CHUNKS : toks - CHUNKS]
        return result, tap[1] * last + tap[2] * prev, tap[2] * last

    own = zbuf.at[z]
    loads[3].wait()
    key_short, q0, q1 = short(1, key_v)
    own[16:17, :] = key_short[0:1]
    own[17:18, :] = key_short[CHUNKS : CHUNKS + 1]
    own[20:21, :] = q0
    own[21:22, :] = q1
    loads[4].wait()
    value_short, q0, q1 = short(2, value_v)
    own[18:19, :] = value_short[0:1]
    own[19:20, :] = value_short[CHUNKS : CHUNKS + 1]
    own[22:23, :] = q0
    own[23:24, :] = q1
    u_ref[...] = rounded(key_short * value_short)
    for n in range(2):
        u_ref[n * CHUNKS : n * CHUNKS + 1, :] = jnp.zeros((1, chans), F32)

    follows = jnp.where((z == NZ - 1) & (x < nx - 1), 1, 0)
    pl.semaphore_wait(barrier, len(near) + 1 + z + (nx - 1 - x) + follows)

    k3 = lax.broadcasted_iota(jnp.int32, (MODES, CHUNKS, LANES), 1)
    for h in range(halves):
        lanes = slice(h * LANES, (h + 1) * LANES)
        a = a_own[:, :, lanes]

        def scan(i, state):
            u = u_ref[pl.ds(pl.multiple_of(i * CHUNKS, CHUNKS), CHUNKS), lanes]
            return state * a + u[None]

        state = lax.fori_loop(0, blocks, scan, jnp.zeros((MODES, CHUNKS, LANES), F32), unroll=8)
        step = a
        for _ in range(int(math.log2(blocks))):
            step = step * step
        shift = 1
        while shift < CHUNKS:
            moved = jnp.where(k3 >= shift, pltpu.roll(state, shift, 1), 0.0)
            state = state + step * moved
            step = step * step
            shift *= 2
        cin[:, :, lanes] = jnp.where(k3 >= 1, pltpu.roll(state, 1, 1), 0.0)
        for s in range(MODES):
            own[s : s + 1, lanes] = state[s, CHUNKS - 1 : CHUNKS, :]

    def send_state(d):
        send(own, own, z_s.at[d - 1], z_r.at[d - 1], (along_z(d), chan))

    def send_edge():
        send(gate_edge, edge, edge_s.at[0], edge_r.at[0], (seq + 1, chan))

    def send_lower(n):
        d = NZ + n - z
        send(own, own, z_s.at[d - 1], z_r.at[d - 1], (x * NZ + n, chan))

    for n in sorted(range(NZ - 1), key=lambda n: (n + 2) % 3 + 3 * (n // 3)):
        pl.when(z > n)(functools.partial(send_lower, n))

    def hello(d):
        pl.semaphore_signal(
            hello_sem.at[d - 1], inc=1, device_id=(seq - d, chan), device_id_type=MESH
        )

    for d in range(1, NZ):
        pl.when(z >= d)(functools.partial(hello, d))

    for copy in own_weights:
        copy.start()

    def origin(way, dist):
        return (y + (2 * way - 1) * dist + ny) % ny

    def pass_on(gather, way, src, item, to=None):
        routes, parts, side, ssem, rsem = gather
        for at, hop, dist in routes:
            if at == src and (dist < half or way == side(item)) and to in (None, dist):
                for ref, n in parts(origin(way, src), item):
                    sem = (way, dist - 1, n)
                    send(ref, ref, ssem.at[sem], rsem.at[sem], (seq, along_y((1 - 2 * way) * hop)))

    def arrive(gather, dist, items):
        _, parts, side, _, rsem = gather
        for item in items:
            for way in range(2):
                if dist < half or way == side(item):
                    for ref, n in parts(origin(way, dist), item):
                        landed(ref, rsem.at[way, dist - 1, n])
                    pass_on(gather, way, dist, item)

    def all_left(gather, items):
        routes, parts, side, ssem, _ = gather
        for _, _, dist in routes:
            for item in items:
                for way in range(2):
                    if dist < half or way == side(item):
                        for ref, n in parts(y, item):
                            left(ref, ssem.at[way, dist - 1, n])

    GATE, LOCAL = 0, 1

    def early_parts(b, item):
        if item == GATE:
            return (modes.at[b], 2), (early.at[GATE, b], GATE)
        return ((early.at[LOCAL, b], LOCAL),)

    first = (ring, early_parts, lambda item: item, early_s, early_r)

    loads[5].wait()
    gate_short, q0, q1 = short(0, gate_v)
    gate_edge[0:1, :] = q0
    gate_edge[1:2, :] = q1
    gate_edge[2:8, :] = jnp.zeros((6, chans), F32)
    pl.when((z == NZ - 1) & (x < nx - 1))(send_edge)
    early[GATE, y] = gate_short[:, 0:LANES].astype(BF16)
    gs_ref[...] = gate_short[:, LANES:]
    for way in range(2):
        pass_on(first, way, 0, GATE)

    loads[6].wait()
    for h in range(halves):
        lanes = slice(h * LANES, (h + 1) * LANES)
        a = a_own[:, :, lanes]
        w = jnp.stack([jnp.broadcast_to(w_v[s : s + 1, lanes], (CHUNKS, LANES)) for s in range(MODES)])
        gain = gain_v[:, lanes]

        def local(i, state):
            both = []
            for n in range(2):
                rows = pl.ds(pl.multiple_of((2 * i + n) * CHUNKS, CHUNKS), CHUNKS)
                u = u_ref[rows, lanes]
                state = state * a + u[None]
                both.append(jnp.sum(state * w, axis=0) + gain * u)
            rows = pl.ds(pl.multiple_of(i * 2 * CHUNKS, 2 * CHUNKS), 2 * CHUNKS)
            if h == 0:
                early[LOCAL, y, rows, :] = jnp.concatenate(both).astype(BF16)
            else:
                y_ref[rows, :] = jnp.concatenate(both)
            return state

        lax.fori_loop(0, blocks // 2, local, cin[:, :, lanes], unroll=2)
        if h == 0:
            for way in range(2):
                pass_on(first, way, 0, LOCAL)
    for s in range(MODES):
        rate = jnp.broadcast_to(rates_v[s : s + 1, :], (CHUNKS, chans))
        lead_own[s] = jnp.broadcast_to(w_v[s : s + 1, :], (CHUNKS, chans)) * jnp.exp(-rate * k8)

    for b in range(ny):
        send(columns(b, 1 - core), held(b, 1), sib_s.at[b], sib_r.at[b], (seq, sibling))

    def gather_first(dists):
        for dist in dists:
            arrive(first, dist, (GATE, LOCAL))
            for way in range(2 if dist < half else 1):
                leads(origin(way, dist))

    gather_first(range(1, min(half, 3)))

    def decay(count):
        return jnp.exp(-r_c * count)

    def edge_tokens(q, msg):
        u0 = rounded((msg[16:17] + q[0:1]) * (msg[18:19] + q[2:3]))
        u1 = rounded((msg[17:18] + q[1:2]) * (msg[19:20] + q[3:4]))
        return u0, u1

    top = lax.broadcasted_iota(jnp.int32, (CHUNKS, LANES), 0) == 0

    def rebuild(a, lead, found, conv_of, gate_of, dst, exact, between=None):
        start = jnp.stack(
            [jnp.broadcast_to(found(s), (CHUNKS, LANES)) * lead(s) for s in range(MODES)]
        )
        edges = [found(MODES + n) for n in range(4)]

        def finish(i, state, first_rows=False):
            rows = pl.ds(pl.multiple_of(i * 2 * CHUNKS, 2 * CHUNKS), 2 * CHUNKS)
            conv, gate = conv_of(rows).astype(F32), gate_of(rows).astype(F32)
            both = []
            for n in range(2):
                part = slice(n * CHUNKS, (n + 1) * CHUNKS)
                total, scale = conv[part] + jnp.sum(state, axis=0), gate[part]
                if first_rows:
                    total = total + jnp.where(top, edges[n], 0.0)
                    scale = scale + jnp.where(top, edges[2 + n], 0.0)
                both.append(scale * (rounded(total) if exact else total))
                state = state * a
            dst(rows, jnp.concatenate(both).astype(BF16))
            return state

        state = lax.fori_loop(1, blocks // 4, finish, finish(0, start, True), unroll=True)
        if between is not None:
            between()
        lax.fori_loop(blocks // 4, blocks // 2, finish, state, unroll=True)

    def store(b, lanes):
        def put(rows, value):
            gathered[b, rows, lanes] = value

        return put

    pieces = toks // 2

    def late_parts(b, item):
        if item == 0:
            return ((late.at[b], 0),)
        rows = pl.ds((item - 1) * pieces, pieces)
        return ((gathered.at[b, rows, pl.ds(LANES, LANES)], item),)

    second = (steps, late_parts, lambda item: item // 2, late_s, late_r)

    back = jnp.exp(r_c)
    early_token = jnp.sum(w_c * back, axis=0, keepdims=True)

    def launch(state_in, q, halo):
        u0, u1 = edge_tokens(q, own[...])
        gain = gain_v[...]
        states[0:MODES, :] = state_in + back * u0 + back * back * u1
        states[16:17, :] = gain * u0 - early_token * u1
        states[17:18, :] = gain * u1
        states[18:20, :] = halo
        states[20:LATE, :] = jnp.zeros((LATE - 20, chans), F32)
        late[y] = states[:, 0:LANES]

        def pass_own(item, to):
            for way in range(2):
                pass_on(second, way, 0, item, to)

        far = steps[0][2]
        pass_own(0, far)
        whole = slice(LANES, 2 * LANES)
        rebuild(
            a_own[:, :, whole],
            lambda s: lead_own[s, :, whole],
            lambda s: states[s : s + 1, whole],
            lambda rows: y_ref[rows, :],
            lambda rows: gs_ref[rows, :],
            store(y, whole),
            True,
            lambda: pass_own(1, far),
        )

        pass_own(2, far)
        if far > 1:
            for item in range(3):
                pass_own(item, 1)

    def launch_first():
        launch(jnp.zeros((MODES, chans), F32), jnp.zeros((4, chans), F32), jnp.zeros((2, chans), F32))

    pl.when(seq == 0)(launch_first)

    span = float(toks)
    d0, d1, d2 = decay(span), decay(span - 1.0), decay(span - 2.0)
    ahead = z.astype(F32) * span
    a0, a1, a2 = decay(ahead), decay(ahead - 1.0), decay(ahead - 2.0)
    e0, e1, e2 = decay(NZ * span), decay(NZ * span - 1.0), decay(NZ * span - 2.0)

    def send_higher(d):
        pl.semaphore_wait(hello_sem.at[d - 1], 1)
        send_state(d)
        if d == 1:
            send_edge()

    for d in range(1, NZ):
        pl.when(z + d < NZ)(functools.partial(send_higher, d))

    def state_of(n):
        landed(zbuf.at[n], z_r.at[(z - n + NZ - 1) % NZ])

    pl.when(z != 0)(functools.partial(state_of, 0))
    msg = zbuf[0]
    cur, q = msg[:MODES], msg[20:24]
    mine, mine_q = jnp.zeros((MODES, chans), F32), jnp.zeros((4, chans), F32)
    for n in range(1, NZ):
        here = z == n
        mine = jnp.where(here, cur, mine)
        mine_q = jnp.where(here, q, mine_q)
        pl.when(z != n)(functools.partial(state_of, n))
        msg = zbuf[n]
        u0, u1 = edge_tokens(q, msg)
        cur = d0 * cur + msg[:MODES] + d1 * u0 + d2 * u1
        q = msg[20:24]
    tmsg[0:MODES, :] = cur
    tmsg[16:20, :] = zbuf[0, 16:20, :]
    tmsg[20:24, :] = q

    def send_total(d):
        send(tmsg, xbuf.at[x], x_s.at[d - 1], x_r.at[d - 1], (seq + d * NZ, chan))

    for d in range(1, nx):
        pl.when(x + d < nx)(functools.partial(send_total, d))

    gather_first(range(3, half))

    carry[...] = jnp.zeros_like(carry)
    last_q[...] = jnp.zeros_like(last_q)

    def fold(n):
        landed(xbuf.at[n], x_r.at[x - n - 1])
        msg = xbuf[n]
        u0, u1 = edge_tokens(last_q[0:4, :], msg)
        carry[...] = e0 * carry[...] + msg[:MODES] + e1 * u0 + e2 * u1
        last_q[0:4, :] = msg[20:24]

    for n in range(nx - 1):
        pl.when(n < x)(functools.partial(fold, n))
    def rest():
        cur, q = carry[...], last_q[0:4, :]
        u0, u1 = edge_tokens(q, zbuf[0])
        inside = mine + a0 * cur + a1 * u0 + a2 * u1
        at_first = z == 0
        state_in = jnp.where(at_first, cur, inside)
        q = jnp.where(at_first, q, mine_q)
        landed(edge, edge_r.at[0])
        launch(state_in, q, edge[0:2, :])

    pl.when(seq > 0)(rest)

    def slots(dist):
        return sorted({dist, ny - dist}) if dist else [0]

    def first_half(dist):
        for d in slots(dist):
            b = (y + d) % ny
            rebuild(
                a_rep[b] if d else a_own[:, :, 0:LANES],
                (lambda s: lead_rep[b, s]) if d else (lambda s: lead_own[s, :, 0:LANES]),
                lambda s: late[b, s : s + 1, :],
                lambda rows: early[LOCAL, b, rows, :],
                lambda rows: early[GATE, b, rows, :],
                store(b, slice(0, LANES)),
                False,
            )

    def product(dists, of):
        total = None
        for dist in dists:
            for d in slots(dist):
                b = (y + d) % ny
                cols = pl.ds(pl.multiple_of(b * chans, chans), chans)
                term = nt(weight_v[of * rows_w : (of + 1) * rows_w, cols], gathered[b])
                total = term if total is None else total + term
        return total

    def add(dists):
        for of in range(2):
            acc[of] += product(dists, of)

    for b in range(ny):
        own_weights[b].wait()
        landed(held(b, 1), sib_r.at[b])
    first_half(0)
    for of in range(2):
        acc[of] = product([0], of)
    if half == 4:
        arrive(second, 2, (0, 1, 2))
        first_half(2)
        arrive(second, 1, (0, 1, 2))
        first_half(1)
        add([1, 2])
        arrive(second, 3, (0,))
        first_half(3)
        gather_first([4])
        arrive(second, 4, (0,))
        first_half(4)
        arrive(second, 3, (1, 2))
        add([3])
        arrive(second, 4, (1, 2))
        last = [4]
    else:
        gather_first([half])
        for dist in range(1, half + 1):
            arrive(second, dist, (0, 1, 2))
            first_half(dist)
        last = list(range(1, half + 1))
    acc[1] += product(last, 1)
    send(acc.at[1], other_acc, sum_s.at[0], sum_r.at[0], (seq, sibling))
    acc[0] += product(last, 0)
    landed(other_acc, sum_r.at[0])
    acc[0] += other_acc[...]
    out_ref[...] = jnp.dot(acc[0].astype(BF16), perm[...], preferred_element_type=F32).astype(BF16)

    for d in range(1, NZ):
        left(own, z_s.at[d - 1])
    for d in range(1, nx):
        pl.when(x + d < nx)(functools.partial(left, tmsg, x_s.at[d - 1]))
    pl.when(seq < nseq - 1)(functools.partial(left, gate_edge, edge_s.at[0]))
    all_left(first, (GATE, LOCAL))
    all_left(second, (0, 1, 2))
    for b in range(ny):
        left(columns(b, 1 - core), sib_s.at[b])
    left(acc.at[1], sum_s.at[0])


def body(nseq, nchan, gate, key, value, taps, gain, rates, residues, weight):
    chans, toks = gate.shape
    nx, ny = nseq // NZ, nchan // 2
    vmem = pl.BlockSpec(memory_space=pltpu.VMEM)
    anywhere = pl.BlockSpec(memory_space=pl.ANY)
    dma = pltpu.SemaphoreType.DMA
    return pl.pallas_call(
        functools.partial(kernel, nseq, nchan),
        out_shape=pltpu.VMEM((weight.shape[0], toks), BF16),
        in_specs=[anywhere] * 8,
        out_specs=vmem,
        scratch_shapes=[
            pltpu.VMEM(taps.shape, F32),
            pltpu.VMEM((1, chans), F32),
            pltpu.VMEM((MODES, chans), F32),
            pltpu.VMEM((MODES, chans), F32),
            pltpu.VMEM((chans, toks), BF16),
            pltpu.VMEM((chans, toks), BF16),
            pltpu.VMEM((chans, toks), BF16),
            pltpu.VMEM((2 * weight.shape[0], weight.shape[1] // 2), BF16),
            pltpu.VMEM((toks, toks), BF16),
            pltpu.VMEM((toks + 2 * CHUNKS, chans), F32),
            pltpu.VMEM((toks, chans), F32),
            pltpu.VMEM((toks, LANES), F32),
            pltpu.VMEM((toks, LANES), F32),
            pltpu.VMEM((MODES, CHUNKS, chans), F32),
            pltpu.VMEM((NZ, MSG, chans), F32),
            pltpu.VMEM((nx, MSG, chans), F32),
            pltpu.VMEM((MSG, chans), F32),
            pltpu.VMEM((MODES, chans), F32),
            pltpu.VMEM((8, chans), F32),
            pltpu.VMEM((8, chans), F32),
            pltpu.VMEM((8, chans), F32),
            pltpu.VMEM((MODES, chans), F32),
            pltpu.VMEM((MODES, CHUNKS, chans), F32),
            pltpu.VMEM((MODES, CHUNKS, chans), F32),
            pltpu.VMEM((LATE, chans), F32),
            pltpu.VMEM((2, ny, toks, LANES), BF16),
            pltpu.VMEM((ny, 2 * MODES, LANES), F32),
            pltpu.VMEM((ny, LATE, LANES), F32),
            pltpu.VMEM((ny, MODES, CHUNKS, LANES), F32),
            pltpu.VMEM((ny, MODES, CHUNKS, LANES), F32),
            pltpu.VMEM((ny, toks, chans), BF16),
            pltpu.VMEM((2, weight.shape[0], toks), F32),
            pltpu.VMEM((weight.shape[0], toks), F32),
            dma((7,)),
            dma((max(NZ - 1, 1),)),
            dma((max(NZ - 1, 1),)),
            dma((max(nx - 1, 1),)),
            dma((max(nx - 1, 1),)),
            dma((2, ny // 2, 3)),
            dma((2, ny // 2, 3)),
            dma((2, ny // 2, 3)),
            dma((2, ny // 2, 3)),
            dma((ny,)),
            dma((ny,)),
            dma((ny,)),
            dma((1,)),
            dma((1,)),
            dma((1,)),
            dma((1,)),
            pltpu.SemaphoreType.REGULAR((max(NZ - 1, 1),)),
        ],
        compiler_params=pltpu.CompilerParams(
            collective_id=0, has_side_effects=True, vmem_limit_bytes=60 * 1024 * 1024
        ),
        name="hyena",
    )(gate, key, value, taps, gain.reshape(1, -1), rates.T, residues.T, weight)


def solution(mesh):
    in_specs = (
        P("chan", "seq"),
        P("chan", "seq"),
        P("chan", "seq"),
        P(None, "chan"),
        P("chan"),
        P("chan", None),
        P("chan", None),
        P("chan", None),
    )
    return jax.shard_map(
        functools.partial(body, mesh.shape["seq"], mesh.shape["chan"]),
        mesh=mesh,
        in_specs=in_specs,
        out_specs=P("chan", "seq"),
        check_vma=False,
    )
```

```python
import functools
import math

import jax
import jax.numpy as jnp
from jax import lax
from jax.experimental import pallas as pl
from jax.experimental.pallas import tpu as pltpu
from jax.sharding import PartitionSpec as P

MESH = pl.DeviceIdType.MESH
F32 = jnp.float32
BF16 = jnp.bfloat16
NZ = 8
MODES = 16
CHUNKS = 8
LANES = 128
MSG = 24
LATE = 24


def rounded(value):
    return value.astype(BF16).astype(F32)


def nt(lhs, rhs):
    return lax.dot_general(lhs, rhs, (((1,), (1,)), ((), ())), preferred_element_type=F32)


def kernel(
    nseq,
    nchan,
    gate_hbm,
    key_hbm,
    value_hbm,
    taps_hbm,
    gain_hbm,
    rates_hbm,
    res_hbm,
    weight_hbm,
    out_ref,
    taps_v,
    gain_v,
    rates_v,
    res_v,
    gate_v,
    key_v,
    value_v,
    weight_v,
    perm,
    ext,
    u_ref,
    gs_ref,
    y_ref,
    cin,
    zbuf,
    xbuf,
    tmsg,
    carry,
    last_q,
    gate_edge,
    edge,
    w_v,
    a_own,
    lead_own,
    states,
    early,
    modes,
    late,
    a_rep,
    lead_rep,
    gathered,
    acc,
    total,
    other_acc,
    in_sem,
    z_s,
    z_r,
    x_s,
    x_r,
    early_s,
    early_r,
    late_s,
    late_r,
    own_w,
    sib_s,
    sib_r,
    sum_s,
    sum_r,
    edge_s,
    edge_r,
    hello_sem,
):
    nx = nseq // NZ
    ny = nchan // 2
    half = ny // 2
    toks = gate_v.shape[1]
    chans = gate_v.shape[0]
    blocks = toks // CHUNKS
    halves = chans // LANES
    seq = lax.axis_index("seq")
    chan = lax.axis_index("chan")
    x, z = seq // NZ, seq % NZ
    y, core = chan // 2, chan % 2
    sibling = chan + 1 - 2 * core

    loads = []
    for n, (src, dst) in enumerate(
        (
            (rates_hbm, rates_v),
            (res_hbm, res_v),
            (taps_hbm, taps_v),
            (key_hbm, key_v),
            (value_hbm, value_v),
            (gate_hbm, gate_v),
            (gain_hbm, gain_v),
        )
    ):
        copy = pltpu.make_async_copy(src, dst, in_sem.at[n])
        copy.start()
        loads.append(copy)

    rows_w = weight_hbm.shape[0]

    def columns(b, of):
        return weight_hbm.at[:, pl.ds(pl.multiple_of((2 * b + of) * chans, chans), chans)]

    def held(b, of):
        return weight_v.at[pl.ds(of * rows_w, rows_w), pl.ds(b * chans, chans)]

    own_weights = [pltpu.make_async_copy(columns(b, core), held(b, 0), own_w.at[b]) for b in range(ny)]
    def along_y(d):
        return ((y + d + ny) % ny) * 2 + core

    def along_z(d):
        return x * NZ + (z + d) % NZ

    barrier = pltpu.get_barrier_semaphore()

    def greet(peer):
        pl.semaphore_signal(barrier, inc=1, device_id=peer, device_id_type=MESH)

    ring = [(dist, 1, dist + 1) for dist in range(half)]
    steps = [(0, 2, 2), (0, 1, 1), (2, 2, 4), (2, 1, 3)] if half == 4 else ring
    near = sorted({way * hop % ny for _, hop, _ in ring + steps for way in (1, -1)})
    for d in near:
        greet((seq, along_y(d)))
    greet((seq, sibling))
    pl.when((z == 0) & (x > 0))(functools.partial(greet, (seq - 1, chan)))
    for d in range(1, NZ):
        pl.when(z + d < NZ)(functools.partial(greet, (seq + d, chan)))
    for d in range(1, nx):
        pl.when(x >= d)(functools.partial(greet, (seq - d * NZ, chan)))

    def send(src, dst, ssem, rsem, peer):
        pltpu.make_async_remote_copy(
            src_ref=src,
            dst_ref=dst,
            send_sem=ssem,
            recv_sem=rsem,
            device_id=peer,
            device_id_type=MESH,
        ).start()

    def landing(ref, ssem, rsem):
        return pltpu.make_async_remote_copy(
            src_ref=ref,
            dst_ref=ref,
            send_sem=ssem,
            recv_sem=rsem,
            device_id=(seq, chan),
            device_id_type=MESH,
        )

    def landed(ref, rsem):
        landing(ref, in_sem.at[0], rsem).wait_recv()

    def left(ref, ssem):
        landing(ref, ssem, in_sem.at[0]).wait_send()

    row = lax.broadcasted_iota(jnp.int32, (toks, toks), 0)
    col = lax.broadcasted_iota(jnp.int32, (toks, toks), 1)
    perm[...] = jnp.where(col == (row % CHUNKS) * blocks + row // CHUNKS, 1.0, 0.0).astype(BF16)
    k8 = lax.broadcasted_iota(jnp.int32, (CHUNKS, chans), 0).astype(F32) * float(blocks) + 1.0
    loads[0].wait()
    loads[1].wait()
    r_c = rates_v[...]
    w_c = res_v[...] * jnp.sqrt(r_c)
    w_v[...] = w_c
    modes[y, 0:MODES, :] = r_c[:, 0:LANES]
    modes[y, MODES:, :] = w_c[:, 0:LANES]
    for s in range(MODES):
        a_own[s] = jnp.exp(-jnp.broadcast_to(rates_v[s : s + 1, :], (CHUNKS, chans)))

    def leads(b):
        for s in range(MODES):
            rate = jnp.broadcast_to(modes[b, s : s + 1, :], (CHUNKS, LANES))
            weight = jnp.broadcast_to(modes[b, MODES + s : MODES + s + 1, :], (CHUNKS, LANES))
            a_rep[b, s] = jnp.exp(-rate)
            lead_rep[b, s] = weight * jnp.exp(-rate * k8[:, 0:LANES])

    at_k0 = lax.broadcasted_iota(jnp.int32, (CHUNKS, chans), 0) == 0
    tail = CHUNKS * (blocks - 2)
    loads[2].wait()

    def taps_of(m):
        return [taps_v[3 * m + j : 3 * m + j + 1, :] for j in range(3)]

    def short(m, source):
        laid = nt(perm[...], source[...])
        tap = taps_of(m)
        ext[2 * CHUNKS :, :] = laid
        for n in range(2):
            block = laid[tail + n * CHUNKS : tail + (n + 1) * CHUNKS]
            ext[n * CHUNKS : (n + 1) * CHUNKS, :] = jnp.where(at_k0, 0.0, pltpu.roll(block, 1, 0))
        result = tap[0] * laid
        result = result + tap[1] * ext[CHUNKS : CHUNKS + toks, :]
        result = result + tap[2] * ext[0:toks, :]
        last = laid[toks - 1 : toks]
        prev = laid[toks - 1 - CHUNKS : toks - CHUNKS]
        return result, tap[1] * last + tap[2] * prev, tap[2] * last

    own = zbuf.at[z]
    loads[3].wait()
    key_short, q0, q1 = short(1, key_v)
    own[16:17, :] = key_short[0:1]
    own[17:18, :] = key_short[CHUNKS : CHUNKS + 1]
    own[20:21, :] = q0
    own[21:22, :] = q1
    loads[4].wait()
    value_short, q0, q1 = short(2, value_v)
    own[18:19, :] = value_short[0:1]
    own[19:20, :] = value_short[CHUNKS : CHUNKS + 1]
    own[22:23, :] = q0
    own[23:24, :] = q1
    u_ref[...] = rounded(key_short * value_short)
    for n in range(2):
        u_ref[n * CHUNKS : n * CHUNKS + 1, :] = jnp.zeros((1, chans), F32)

    follows = jnp.where((z == NZ - 1) & (x < nx - 1), 1, 0)
    pl.semaphore_wait(barrier, len(near) + 1 + z + (nx - 1 - x) + follows)

    k3 = lax.broadcasted_iota(jnp.int32, (MODES, CHUNKS, LANES), 1)
    for h in range(halves):
        lanes = slice(h * LANES, (h + 1) * LANES)
        a = a_own[:, :, lanes]

        def scan(i, state):
            u = u_ref[pl.ds(pl.multiple_of(i * CHUNKS, CHUNKS), CHUNKS), lanes]
            return state * a + u[None]

        state = lax.fori_loop(0, blocks, scan, jnp.zeros((MODES, CHUNKS, LANES), F32), unroll=8)
        step = a
        for _ in range(int(math.log2(blocks))):
            step = step * step
        shift = 1
        while shift < CHUNKS:
            moved = jnp.where(k3 >= shift, pltpu.roll(state, shift, 1), 0.0)
            state = state + step * moved
            step = step * step
            shift *= 2
        cin[:, :, lanes] = jnp.where(k3 >= 1, pltpu.roll(state, 1, 1), 0.0)
        for s in range(MODES):
            own[s : s + 1, lanes] = state[s, CHUNKS - 1 : CHUNKS, :]

    def send_state(d):
        send(own, own, z_s.at[d - 1], z_r.at[d - 1], (along_z(d), chan))

    def send_edge():
        send(gate_edge, edge, edge_s.at[0], edge_r.at[0], (seq + 1, chan))

    def send_lower(n):
        d = NZ + n - z
        send(own, own, z_s.at[d - 1], z_r.at[d - 1], (x * NZ + n, chan))

    for n in sorted(range(NZ - 1), key=lambda n: (n + 2) % 3 + 3 * (n // 3)):
        pl.when(z > n)(functools.partial(send_lower, n))

    def hello(d):
        pl.semaphore_signal(
            hello_sem.at[d - 1], inc=1, device_id=(seq - d, chan), device_id_type=MESH
        )

    for d in range(1, NZ):
        pl.when(z >= d)(functools.partial(hello, d))

    for copy in own_weights:
        copy.start()

    def origin(way, dist):
        return (y + (2 * way - 1) * dist + ny) % ny

    def pass_on(gather, way, src, item, to=None):
        routes, parts, side, ssem, rsem = gather
        for at, hop, dist in routes:
            if at == src and (dist < half or way == side(item)) and to in (None, dist):
                for ref, n in parts(origin(way, src), item):
                    sem = (way, dist - 1, n)
                    send(ref, ref, ssem.at[sem], rsem.at[sem], (seq, along_y((1 - 2 * way) * hop)))

    def arrive(gather, dist, items):
        _, parts, side, _, rsem = gather
        for item in items:
            for way in range(2):
                if dist < half or way == side(item):
                    for ref, n in parts(origin(way, dist), item):
                        landed(ref, rsem.at[way, dist - 1, n])
                    pass_on(gather, way, dist, item)

    def all_left(gather, items):
        routes, parts, side, ssem, _ = gather
        for _, _, dist in routes:
            for item in items:
                for way in range(2):
                    if dist < half or way == side(item):
                        for ref, n in parts(y, item):
                            left(ref, ssem.at[way, dist - 1, n])

    GATE, LOCAL = 0, 1

    def early_parts(b, item):
        if item == GATE:
            return (modes.at[b], 2), (early.at[GATE, b], GATE)
        return ((early.at[LOCAL, b], LOCAL),)

    first = (ring, early_parts, lambda item: item, early_s, early_r)

    loads[5].wait()
    gate_short, q0, q1 = short(0, gate_v)
    gate_edge[0:1, :] = q0
    gate_edge[1:2, :] = q1
    gate_edge[2:8, :] = jnp.zeros((6, chans), F32)
    pl.when((z == NZ - 1) & (x < nx - 1))(send_edge)
    early[GATE, y] = gate_short[:, 0:LANES].astype(BF16)
    gs_ref[...] = gate_short[:, LANES:]
    for way in range(2):
        pass_on(first, way, 0, GATE)

    loads[6].wait()
    for h in range(halves):
        lanes = slice(h * LANES, (h + 1) * LANES)
        a = a_own[:, :, lanes]
        w = jnp.stack([jnp.broadcast_to(w_v[s : s + 1, lanes], (CHUNKS, LANES)) for s in range(MODES)])
        gain = gain_v[:, lanes]

        def local(i, state):
            both = []
            for n in range(2):
                rows = pl.ds(pl.multiple_of((2 * i + n) * CHUNKS, CHUNKS), CHUNKS)
                u = u_ref[rows, lanes]
                state = state * a + u[None]
                both.append(jnp.sum(state * w, axis=0) + gain * u)
            rows = pl.ds(pl.multiple_of(i * 2 * CHUNKS, 2 * CHUNKS), 2 * CHUNKS)
            if h == 0:
                early[LOCAL, y, rows, :] = jnp.concatenate(both).astype(BF16)
            else:
                y_ref[rows, :] = jnp.concatenate(both)
            return state

        lax.fori_loop(0, blocks // 2, local, cin[:, :, lanes], unroll=2)
        if h == 0:
            for way in range(2):
                pass_on(first, way, 0, LOCAL)
    for s in range(MODES):
        rate = jnp.broadcast_to(rates_v[s : s + 1, :], (CHUNKS, chans))
        lead_own[s] = jnp.broadcast_to(w_v[s : s + 1, :], (CHUNKS, chans)) * jnp.exp(-rate * k8)

    for b in range(ny):
        send(columns(b, 1 - core), held(b, 1), sib_s.at[b], sib_r.at[b], (seq, sibling))

    def gather_first(dists):
        for dist in dists:
            arrive(first, dist, (GATE, LOCAL))
            for way in range(2 if dist < half else 1):
                leads(origin(way, dist))

    gather_first(range(1, min(half, 3)))

    def decay(count):
        return jnp.exp(-r_c * count)

    def edge_tokens(q, msg):
        u0 = rounded((msg[16:17] + q[0:1]) * (msg[18:19] + q[2:3]))
        u1 = rounded((msg[17:18] + q[1:2]) * (msg[19:20] + q[3:4]))
        return u0, u1

    top = lax.broadcasted_iota(jnp.int32, (CHUNKS, LANES), 0) == 0

    def rebuild(a, lead, found, conv_of, gate_of, dst, exact, between=None):
        start = jnp.stack(
            [jnp.broadcast_to(found(s), (CHUNKS, LANES)) * lead(s) for s in range(MODES)]
        )
        edges = [found(MODES + n) for n in range(4)]

        def finish(i, state, first_rows=False):
            rows = pl.ds(pl.multiple_of(i * 2 * CHUNKS, 2 * CHUNKS), 2 * CHUNKS)
            conv, gate = conv_of(rows).astype(F32), gate_of(rows).astype(F32)
            both = []
            for n in range(2):
                part = slice(n * CHUNKS, (n + 1) * CHUNKS)
                total, scale = conv[part] + jnp.sum(state, axis=0), gate[part]
                if first_rows:
                    total = total + jnp.where(top, edges[n], 0.0)
                    scale = scale + jnp.where(top, edges[2 + n], 0.0)
                both.append(scale * (rounded(total) if exact else total))
                state = state * a
            dst(rows, jnp.concatenate(both).astype(BF16))
            return state

        state = lax.fori_loop(1, blocks // 4, finish, finish(0, start, True), unroll=True)
        if between is not None:
            between()
        lax.fori_loop(blocks // 4, blocks // 2, finish, state, unroll=True)

    def store(b, lanes):
        def put(rows, value):
            gathered[b, rows, lanes] = value

        return put

    pieces = toks // 2

    def late_parts(b, item):
        if item == 0:
            return ((late.at[b], 0),)
        rows = pl.ds((item - 1) * pieces, pieces)
        return ((gathered.at[b, rows, pl.ds(LANES, LANES)], item),)

    second = (steps, late_parts, lambda item: item // 2, late_s, late_r)

    back = jnp.exp(r_c)
    early_token = jnp.sum(w_c * back, axis=0, keepdims=True)

    def launch(state_in, q, halo):
        u0, u1 = edge_tokens(q, own[...])
        gain = gain_v[...]
        states[0:MODES, :] = state_in + back * u0 + back * back * u1
        states[16:17, :] = gain * u0 - early_token * u1
        states[17:18, :] = gain * u1
        states[18:20, :] = halo
        states[20:LATE, :] = jnp.zeros((LATE - 20, chans), F32)
        late[y] = states[:, 0:LANES]

        def pass_own(item, to):
            for way in range(2):
                pass_on(second, way, 0, item, to)

        far = steps[0][2]
        pass_own(0, far)
        whole = slice(LANES, 2 * LANES)
        rebuild(
            a_own[:, :, whole],
            lambda s: lead_own[s, :, whole],
            lambda s: states[s : s + 1, whole],
            lambda rows: y_ref[rows, :],
            lambda rows: gs_ref[rows, :],
            store(y, whole),
            True,
            lambda: pass_own(1, far),
        )

        pass_own(2, far)
        if far > 1:
            for item in range(3):
                pass_own(item, 1)

    def launch_first():
        launch(jnp.zeros((MODES, chans), F32), jnp.zeros((4, chans), F32), jnp.zeros((2, chans), F32))

    pl.when(seq == 0)(launch_first)

    span = float(toks)
    d0, d1, d2 = decay(span), decay(span - 1.0), decay(span - 2.0)
    ahead = z.astype(F32) * span
    a0, a1, a2 = decay(ahead), decay(ahead - 1.0), decay(ahead - 2.0)
    e0, e1, e2 = decay(NZ * span), decay(NZ * span - 1.0), decay(NZ * span - 2.0)

    def send_higher(d):
        pl.semaphore_wait(hello_sem.at[d - 1], 1)
        send_state(d)
        if d == 1:
            send_edge()

    for d in range(1, NZ):
        pl.when(z + d < NZ)(functools.partial(send_higher, d))

    def state_of(n):
        landed(zbuf.at[n], z_r.at[(z - n + NZ - 1) % NZ])

    pl.when(z != 0)(functools.partial(state_of, 0))
    msg = zbuf[0]
    cur, q = msg[:MODES], msg[20:24]
    mine, mine_q = jnp.zeros((MODES, chans), F32), jnp.zeros((4, chans), F32)
    for n in range(1, NZ):
        here = z == n
        mine = jnp.where(here, cur, mine)
        mine_q = jnp.where(here, q, mine_q)
        pl.when(z != n)(functools.partial(state_of, n))
        msg = zbuf[n]
        u0, u1 = edge_tokens(q, msg)
        cur = d0 * cur + msg[:MODES] + d1 * u0 + d2 * u1
        q = msg[20:24]
    tmsg[0:MODES, :] = cur
    tmsg[16:20, :] = zbuf[0, 16:20, :]
    tmsg[20:24, :] = q

    def send_total(d):
        send(tmsg, xbuf.at[x], x_s.at[d - 1], x_r.at[d - 1], (seq + d * NZ, chan))

    for d in range(1, nx):
        pl.when(x + d < nx)(functools.partial(send_total, d))

    gather_first(range(3, half))

    carry[...] = jnp.zeros_like(carry)
    last_q[...] = jnp.zeros_like(last_q)

    def fold(n):
        landed(xbuf.at[n], x_r.at[x - n - 1])
        msg = xbuf[n]
        u0, u1 = edge_tokens(last_q[0:4, :], msg)
        carry[...] = e0 * carry[...] + msg[:MODES] + e1 * u0 + e2 * u1
        last_q[0:4, :] = msg[20:24]

    for n in range(nx - 1):
        pl.when(n < x)(functools.partial(fold, n))
    def rest():
        cur, q = carry[...], last_q[0:4, :]
        u0, u1 = edge_tokens(q, zbuf[0])
        inside = mine + a0 * cur + a1 * u0 + a2 * u1
        at_first = z == 0
        state_in = jnp.where(at_first, cur, inside)
        q = jnp.where(at_first, q, mine_q)
        landed(edge, edge_r.at[0])
        launch(state_in, q, edge[0:2, :])

    pl.when(seq > 0)(rest)

    def slots(dist):
        return sorted({dist, ny - dist}) if dist else [0]

    def first_half(dist):
        for d in slots(dist):
            b = (y + d) % ny
            rebuild(
                a_rep[b] if d else a_own[:, :, 0:LANES],
                (lambda s: lead_rep[b, s]) if d else (lambda s: lead_own[s, :, 0:LANES]),
                lambda s: late[b, s : s + 1, :],
                lambda rows: early[LOCAL, b, rows, :],
                lambda rows: early[GATE, b, rows, :],
                store(b, slice(0, LANES)),
                False,
            )

    def product(dists, of):
        total = None
        for dist in dists:
            for d in slots(dist):
                b = (y + d) % ny
                cols = pl.ds(pl.multiple_of(b * chans, chans), chans)
                term = nt(weight_v[of * rows_w : (of + 1) * rows_w, cols], gathered[b])
                total = term if total is None else total + term
        return total

    def add(dists):
        for of in range(2):
            acc[of] += product(dists, of)

    for b in range(ny):
        own_weights[b].wait()
        landed(held(b, 1), sib_r.at[b])
    first_half(0)
    for of in range(2):
        acc[of] = product([0], of)
    if half == 4:
        arrive(second, 2, (0, 1, 2))
        first_half(2)
        arrive(second, 1, (0, 1, 2))
        first_half(1)
        add([1, 2])
        arrive(second, 3, (0,))
        first_half(3)
        gather_first([4])
        arrive(second, 4, (0,))
        first_half(4)
        arrive(second, 3, (1, 2))
        add([3])
        arrive(second, 4, (1, 2))
        last = [4]
    else:
        gather_first([half])
        for dist in range(1, half + 1):
            arrive(second, dist, (0, 1, 2))
            first_half(dist)
        last = list(range(1, half + 1))
    total[...] = (acc[1] + product(last, 1)).astype(BF16)
    send(total, other_acc, sum_s.at[0], sum_r.at[0], (seq, sibling))
    acc[0] += product(last, 0)
    landed(other_acc, sum_r.at[0])
    acc[0] += other_acc[...].astype(F32)
    out_ref[...] = jnp.dot(acc[0].astype(BF16), perm[...], preferred_element_type=F32).astype(BF16)

    for d in range(1, NZ):
        left(own, z_s.at[d - 1])
    for d in range(1, nx):
        pl.when(x + d < nx)(functools.partial(left, tmsg, x_s.at[d - 1]))
    pl.when(seq < nseq - 1)(functools.partial(left, gate_edge, edge_s.at[0]))
    all_left(first, (GATE, LOCAL))
    all_left(second, (0, 1, 2))
    for b in range(ny):
        left(columns(b, 1 - core), sib_s.at[b])
    left(total, sum_s.at[0])


def body(nseq, nchan, gate, key, value, taps, gain, rates, residues, weight):
    chans, toks = gate.shape
    nx, ny = nseq // NZ, nchan // 2
    vmem = pl.BlockSpec(memory_space=pltpu.VMEM)
    anywhere = pl.BlockSpec(memory_space=pl.ANY)
    dma = pltpu.SemaphoreType.DMA
    return pl.pallas_call(
        functools.partial(kernel, nseq, nchan),
        out_shape=pltpu.VMEM((weight.shape[0], toks), BF16),
        in_specs=[anywhere] * 8,
        out_specs=vmem,
        scratch_shapes=[
            pltpu.VMEM(taps.shape, F32),
            pltpu.VMEM((1, chans), F32),
            pltpu.VMEM((MODES, chans), F32),
            pltpu.VMEM((MODES, chans), F32),
            pltpu.VMEM((chans, toks), BF16),
            pltpu.VMEM((chans, toks), BF16),
            pltpu.VMEM((chans, toks), BF16),
            pltpu.VMEM((2 * weight.shape[0], weight.shape[1] // 2), BF16),
            pltpu.VMEM((toks, toks), BF16),
            pltpu.VMEM((toks + 2 * CHUNKS, chans), F32),
            pltpu.VMEM((toks, chans), F32),
            pltpu.VMEM((toks, LANES), F32),
            pltpu.VMEM((toks, LANES), F32),
            pltpu.VMEM((MODES, CHUNKS, chans), F32),
            pltpu.VMEM((NZ, MSG, chans), F32),
            pltpu.VMEM((nx, MSG, chans), F32),
            pltpu.VMEM((MSG, chans), F32),
            pltpu.VMEM((MODES, chans), F32),
            pltpu.VMEM((8, chans), F32),
            pltpu.VMEM((8, chans), F32),
            pltpu.VMEM((8, chans), F32),
            pltpu.VMEM((MODES, chans), F32),
            pltpu.VMEM((MODES, CHUNKS, chans), F32),
            pltpu.VMEM((MODES, CHUNKS, chans), F32),
            pltpu.VMEM((LATE, chans), F32),
            pltpu.VMEM((2, ny, toks, LANES), BF16),
            pltpu.VMEM((ny, 2 * MODES, LANES), F32),
            pltpu.VMEM((ny, LATE, LANES), F32),
            pltpu.VMEM((ny, MODES, CHUNKS, LANES), F32),
            pltpu.VMEM((ny, MODES, CHUNKS, LANES), F32),
            pltpu.VMEM((ny, toks, chans), BF16),
            pltpu.VMEM((2, weight.shape[0], toks), F32),
            pltpu.VMEM((weight.shape[0], toks), BF16),
            pltpu.VMEM((weight.shape[0], toks), BF16),
            dma((7,)),
            dma((max(NZ - 1, 1),)),
            dma((max(NZ - 1, 1),)),
            dma((max(nx - 1, 1),)),
            dma((max(nx - 1, 1),)),
            dma((2, ny // 2, 3)),
            dma((2, ny // 2, 3)),
            dma((2, ny // 2, 3)),
            dma((2, ny // 2, 3)),
            dma((ny,)),
            dma((ny,)),
            dma((ny,)),
            dma((1,)),
            dma((1,)),
            dma((1,)),
            dma((1,)),
            pltpu.SemaphoreType.REGULAR((max(NZ - 1, 1),)),
        ],
        compiler_params=pltpu.CompilerParams(
            collective_id=0, has_side_effects=True, vmem_limit_bytes=60 * 1024 * 1024
        ),
        name="hyena",
    )(gate, key, value, taps, gain.reshape(1, -1), rates.T, residues.T, weight)


def solution(mesh):
    in_specs = (
        P("chan", "seq"),
        P("chan", "seq"),
        P("chan", "seq"),
        P(None, "chan"),
        P("chan"),
        P("chan", None),
        P("chan", None),
        P("chan", None),
    )
    return jax.shard_map(
        functools.partial(body, mesh.shape["seq"], mesh.shape["chan"]),
        mesh=mesh,
        in_specs=in_specs,
        out_specs=P("chan", "seq"),
        check_vma=False,
    )
```

```python
import functools
import math

import jax
import jax.numpy as jnp
from jax import lax
from jax.experimental import pallas as pl
from jax.experimental.pallas import tpu as pltpu
from jax.sharding import PartitionSpec as P

MESH = pl.DeviceIdType.MESH
F32 = jnp.float32
BF16 = jnp.bfloat16
NZ = 8
MODES = 16
CHUNKS = 8
LANES = 128
MSG = 24
LATE = 24


def rounded(value):
    return value.astype(BF16).astype(F32)


def nt(lhs, rhs):
    return lax.dot_general(lhs, rhs, (((1,), (1,)), ((), ())), preferred_element_type=F32)


def kernel(
    nseq,
    nchan,
    gate_hbm,
    key_hbm,
    value_hbm,
    taps_hbm,
    gain_hbm,
    rates_hbm,
    res_hbm,
    weight_hbm,
    out_ref,
    taps_v,
    gain_v,
    rates_v,
    res_v,
    gate_v,
    key_v,
    value_v,
    weight_v,
    perm,
    ext,
    u_ref,
    gs_ref,
    y_ref,
    cin,
    zbuf,
    xbuf,
    tmsg,
    carry,
    last_q,
    gate_edge,
    edge,
    w_v,
    a_own,
    lead_own,
    states,
    early,
    modes,
    late,
    a_rep,
    lead_rep,
    gathered,
    acc,
    other_acc,
    in_sem,
    z_s,
    z_r,
    x_s,
    x_r,
    early_s,
    early_r,
    late_s,
    late_r,
    own_w,
    sib_s,
    sib_r,
    sum_s,
    sum_r,
    edge_s,
    edge_r,
    hello_sem,
):
    nx = nseq // NZ
    ny = nchan // 2
    half = ny // 2
    toks = gate_v.shape[1]
    chans = gate_v.shape[0]
    blocks = toks // CHUNKS
    halves = chans // LANES
    seq = lax.axis_index("seq")
    chan = lax.axis_index("chan")
    x, z = seq // NZ, seq % NZ
    y, core = chan // 2, chan % 2
    sibling = chan + 1 - 2 * core

    loads = []
    for n, (src, dst) in enumerate(
        (
            (key_hbm, key_v),
            (value_hbm, value_v),
            (rates_hbm, rates_v),
            (res_hbm, res_v),
            (taps_hbm, taps_v),
            (gate_hbm, gate_v),
            (gain_hbm, gain_v),
        )
    ):
        copy = pltpu.make_async_copy(src, dst, in_sem.at[n])
        copy.start()
        loads.append(copy)

    rows_w = weight_hbm.shape[0]

    def columns(b, of):
        return weight_hbm.at[:, pl.ds(pl.multiple_of((2 * b + of) * chans, chans), chans)]

    def held(b, of):
        return weight_v.at[pl.ds(of * rows_w, rows_w), pl.ds(b * chans, chans)]

    own_weights = [pltpu.make_async_copy(columns(b, core), held(b, 0), own_w.at[b]) for b in range(ny)]
    def along_y(d):
        return ((y + d + ny) % ny) * 2 + core

    def along_z(d):
        return x * NZ + (z + d) % NZ

    barrier = pltpu.get_barrier_semaphore()

    def greet(peer):
        pl.semaphore_signal(barrier, inc=1, device_id=peer, device_id_type=MESH)

    ring = [(dist, 1, dist + 1) for dist in range(half)]
    steps = [(0, 2, 2), (0, 1, 1), (2, 2, 4), (2, 1, 3)] if half == 4 else ring
    near = sorted({way * hop % ny for _, hop, _ in ring + steps for way in (1, -1)})
    for d in near:
        greet((seq, along_y(d)))
    greet((seq, sibling))
    pl.when((z == 0) & (x > 0))(functools.partial(greet, (seq - 1, chan)))
    for d in range(1, NZ):
        pl.when(z + d < NZ)(functools.partial(greet, (seq + d, chan)))
    for d in range(1, nx):
        pl.when(x >= d)(functools.partial(greet, (seq - d * NZ, chan)))

    def send(src, dst, ssem, rsem, peer):
        pltpu.make_async_remote_copy(
            src_ref=src,
            dst_ref=dst,
            send_sem=ssem,
            recv_sem=rsem,
            device_id=peer,
            device_id_type=MESH,
        ).start()

    def landing(ref, ssem, rsem):
        return pltpu.make_async_remote_copy(
            src_ref=ref,
            dst_ref=ref,
            send_sem=ssem,
            recv_sem=rsem,
            device_id=(seq, chan),
            device_id_type=MESH,
        )

    def landed(ref, rsem):
        landing(ref, in_sem.at[0], rsem).wait_recv()

    def left(ref, ssem):
        landing(ref, ssem, in_sem.at[0]).wait_send()

    row = lax.broadcasted_iota(jnp.int32, (toks, toks), 0)
    col = lax.broadcasted_iota(jnp.int32, (toks, toks), 1)
    perm[...] = jnp.where(col == (row % CHUNKS) * blocks + row // CHUNKS, 1.0, 0.0).astype(BF16)
    k8 = lax.broadcasted_iota(jnp.int32, (CHUNKS, chans), 0).astype(F32) * float(blocks) + 1.0
    loads[2].wait()
    loads[3].wait()
    r_c = rates_v[...]
    w_c = res_v[...] * jnp.sqrt(r_c)
    w_v[...] = w_c
    modes[y, 0:MODES, :] = r_c[:, 0:LANES]
    modes[y, MODES:, :] = w_c[:, 0:LANES]
    for s in range(MODES):
        a_own[s] = jnp.exp(-jnp.broadcast_to(rates_v[s : s + 1, :], (CHUNKS, chans)))

    def leads(b):
        for s in range(MODES):
            rate = jnp.broadcast_to(modes[b, s : s + 1, :], (CHUNKS, LANES))
            weight = jnp.broadcast_to(modes[b, MODES + s : MODES + s + 1, :], (CHUNKS, LANES))
            a_rep[b, s] = jnp.exp(-rate)
            lead_rep[b, s] = weight * jnp.exp(-rate * k8[:, 0:LANES])

    at_k0 = lax.broadcasted_iota(jnp.int32, (CHUNKS, chans), 0) == 0
    tail = CHUNKS * (blocks - 2)
    loads[4].wait()

    def taps_of(m):
        return [taps_v[3 * m + j : 3 * m + j + 1, :] for j in range(3)]

    def short(m, source):
        laid = nt(perm[...], source[...])
        tap = taps_of(m)
        ext[2 * CHUNKS :, :] = laid
        for n in range(2):
            block = laid[tail + n * CHUNKS : tail + (n + 1) * CHUNKS]
            ext[n * CHUNKS : (n + 1) * CHUNKS, :] = jnp.where(at_k0, 0.0, pltpu.roll(block, 1, 0))
        result = tap[0] * laid
        result = result + tap[1] * ext[CHUNKS : CHUNKS + toks, :]
        result = result + tap[2] * ext[0:toks, :]
        last = laid[toks - 1 : toks]
        prev = laid[toks - 1 - CHUNKS : toks - CHUNKS]
        return result, tap[1] * last + tap[2] * prev, tap[2] * last

    own = zbuf.at[z]
    loads[0].wait()
    key_short, q0, q1 = short(1, key_v)
    own[16:17, :] = key_short[0:1]
    own[17:18, :] = key_short[CHUNKS : CHUNKS + 1]
    own[20:21, :] = q0
    own[21:22, :] = q1
    loads[1].wait()
    value_short, q0, q1 = short(2, value_v)
    own[18:19, :] = value_short[0:1]
    own[19:20, :] = value_short[CHUNKS : CHUNKS + 1]
    own[22:23, :] = q0
    own[23:24, :] = q1
    u_ref[...] = rounded(key_short * value_short)
    for n in range(2):
        u_ref[n * CHUNKS : n * CHUNKS + 1, :] = jnp.zeros((1, chans), F32)

    follows = jnp.where((z == NZ - 1) & (x < nx - 1), 1, 0)
    pl.semaphore_wait(barrier, len(near) + 1 + z + (nx - 1 - x) + follows)

    k3 = lax.broadcasted_iota(jnp.int32, (MODES, CHUNKS, LANES), 1)
    for h in range(halves):
        lanes = slice(h * LANES, (h + 1) * LANES)
        a = a_own[:, :, lanes]

        def scan(i, state):
            u = u_ref[pl.ds(pl.multiple_of(i * CHUNKS, CHUNKS), CHUNKS), lanes]
            return state * a + u[None]

        state = lax.fori_loop(0, blocks, scan, jnp.zeros((MODES, CHUNKS, LANES), F32), unroll=8)
        step = a
        for _ in range(int(math.log2(blocks))):
            step = step * step
        shift = 1
        while shift < CHUNKS:
            moved = jnp.where(k3 >= shift, pltpu.roll(state, shift, 1), 0.0)
            state = state + step * moved
            step = step * step
            shift *= 2
        cin[:, :, lanes] = jnp.where(k3 >= 1, pltpu.roll(state, 1, 1), 0.0)
        for s in range(MODES):
            own[s : s + 1, lanes] = state[s, CHUNKS - 1 : CHUNKS, :]

    def send_state(d):
        send(own, own, z_s.at[d - 1], z_r.at[d - 1], (along_z(d), chan))

    def send_edge():
        send(gate_edge, edge, edge_s.at[0], edge_r.at[0], (seq + 1, chan))

    def send_lower(n):
        d = NZ + n - z
        send(own, own, z_s.at[d - 1], z_r.at[d - 1], (x * NZ + n, chan))

    for n in sorted(range(NZ - 1), key=lambda n: (n + 2) % 3 + 3 * (n // 3)):
        pl.when(z > n)(functools.partial(send_lower, n))

    def hello(d):
        pl.semaphore_signal(
            hello_sem.at[d - 1], inc=1, device_id=(seq - d, chan), device_id_type=MESH
        )

    for d in range(1, NZ):
        pl.when(z >= d)(functools.partial(hello, d))

    for copy in own_weights:
        copy.start()

    def origin(way, dist):
        return (y + (2 * way - 1) * dist + ny) % ny

    def pass_on(gather, way, src, item, to=None):
        routes, parts, side, ssem, rsem = gather
        for at, hop, dist in routes:
            if at == src and (dist < half or way == side(item)) and to in (None, dist):
                for ref, n in parts(origin(way, src), item):
                    sem = (way, dist - 1, n)
                    send(ref, ref, ssem.at[sem], rsem.at[sem], (seq, along_y((1 - 2 * way) * hop)))

    def arrive(gather, dist, items):
        _, parts, side, _, rsem = gather
        for item in items:
            for way in range(2):
                if dist < half or way == side(item):
                    for ref, n in parts(origin(way, dist), item):
                        landed(ref, rsem.at[way, dist - 1, n])
                    pass_on(gather, way, dist, item)

    def all_left(gather, items):
        routes, parts, side, ssem, _ = gather
        for _, _, dist in routes:
            for item in items:
                for way in range(2):
                    if dist < half or way == side(item):
                        for ref, n in parts(y, item):
                            left(ref, ssem.at[way, dist - 1, n])

    GATE, LOCAL = 0, 1

    def early_parts(b, item):
        if item == GATE:
            return (modes.at[b], 2), (early.at[GATE, b], GATE)
        return ((early.at[LOCAL, b], LOCAL),)

    first = (ring, early_parts, lambda item: item, early_s, early_r)

    loads[5].wait()
    gate_short, q0, q1 = short(0, gate_v)
    gate_edge[0:1, :] = q0
    gate_edge[1:2, :] = q1
    gate_edge[2:8, :] = jnp.zeros((6, chans), F32)
    pl.when((z == NZ - 1) & (x < nx - 1))(send_edge)
    early[GATE, y] = gate_short[:, 0:LANES].astype(BF16)
    gs_ref[...] = gate_short[:, LANES:]
    for way in range(2):
        pass_on(first, way, 0, GATE)

    loads[6].wait()
    for h in range(halves):
        lanes = slice(h * LANES, (h + 1) * LANES)
        a = a_own[:, :, lanes]
        w = jnp.stack([jnp.broadcast_to(w_v[s : s + 1, lanes], (CHUNKS, LANES)) for s in range(MODES)])
        gain = gain_v[:, lanes]

        def local(i, state):
            both = []
            for n in range(2):
                rows = pl.ds(pl.multiple_of((2 * i + n) * CHUNKS, CHUNKS), CHUNKS)
                u = u_ref[rows, lanes]
                state = state * a + u[None]
                both.append(jnp.sum(state * w, axis=0) + gain * u)
            rows = pl.ds(pl.multiple_of(i * 2 * CHUNKS, 2 * CHUNKS), 2 * CHUNKS)
            if h == 0:
                early[LOCAL, y, rows, :] = jnp.concatenate(both).astype(BF16)
            else:
                y_ref[rows, :] = jnp.concatenate(both)
            return state

        lax.fori_loop(0, blocks // 2, local, cin[:, :, lanes], unroll=2)
        if h == 0:
            for way in range(2):
                pass_on(first, way, 0, LOCAL)
    for s in range(MODES):
        rate = jnp.broadcast_to(rates_v[s : s + 1, :], (CHUNKS, chans))
        lead_own[s] = jnp.broadcast_to(w_v[s : s + 1, :], (CHUNKS, chans)) * jnp.exp(-rate * k8)

    for b in range(ny):
        send(columns(b, 1 - core), held(b, 1), sib_s.at[b], sib_r.at[b], (seq, sibling))

    def gather_first(dists):
        for dist in dists:
            arrive(first, dist, (GATE, LOCAL))
            for way in range(2 if dist < half else 1):
                leads(origin(way, dist))

    gather_first(range(1, min(half, 3)))

    def decay(count):
        return jnp.exp(-r_c * count)

    def edge_tokens(q, msg):
        u0 = rounded((msg[16:17] + q[0:1]) * (msg[18:19] + q[2:3]))
        u1 = rounded((msg[17:18] + q[1:2]) * (msg[19:20] + q[3:4]))
        return u0, u1

    top = lax.broadcasted_iota(jnp.int32, (CHUNKS, LANES), 0) == 0

    def rebuild(a, lead, found, conv_of, gate_of, dst, exact, between=None):
        start = jnp.stack(
            [jnp.broadcast_to(found(s), (CHUNKS, LANES)) * lead(s) for s in range(MODES)]
        )
        edges = [found(MODES + n) for n in range(4)]

        def finish(i, state, first_rows=False):
            rows = pl.ds(pl.multiple_of(i * 2 * CHUNKS, 2 * CHUNKS), 2 * CHUNKS)
            conv, gate = conv_of(rows).astype(F32), gate_of(rows).astype(F32)
            both = []
            for n in range(2):
                part = slice(n * CHUNKS, (n + 1) * CHUNKS)
                total, scale = conv[part] + jnp.sum(state, axis=0), gate[part]
                if first_rows:
                    total = total + jnp.where(top, edges[n], 0.0)
                    scale = scale + jnp.where(top, edges[2 + n], 0.0)
                both.append(scale * (rounded(total) if exact else total))
                state = state * a
            dst(rows, jnp.concatenate(both).astype(BF16))
            return state

        state = lax.fori_loop(1, blocks // 4, finish, finish(0, start, True), unroll=True)
        if between is not None:
            between()
        lax.fori_loop(blocks // 4, blocks // 2, finish, state, unroll=True)

    def store(b, lanes):
        def put(rows, value):
            gathered[b, rows, lanes] = value

        return put

    pieces = toks // 2

    def late_parts(b, item):
        if item == 0:
            return ((late.at[b], 0),)
        rows = pl.ds((item - 1) * pieces, pieces)
        return ((gathered.at[b, rows, pl.ds(LANES, LANES)], item),)

    second = (steps, late_parts, lambda item: item // 2, late_s, late_r)

    back = jnp.exp(r_c)
    early_token = jnp.sum(w_c * back, axis=0, keepdims=True)

    def launch(state_in, q, halo):
        u0, u1 = edge_tokens(q, own[...])
        gain = gain_v[...]
        states[0:MODES, :] = state_in + back * u0 + back * back * u1
        states[16:17, :] = gain * u0 - early_token * u1
        states[17:18, :] = gain * u1
        states[18:20, :] = halo
        states[20:LATE, :] = jnp.zeros((LATE - 20, chans), F32)
        late[y] = states[:, 0:LANES]

        def pass_own(item, to):
            for way in range(2):
                pass_on(second, way, 0, item, to)

        far = steps[0][2]
        pass_own(0, far)
        whole = slice(LANES, 2 * LANES)
        rebuild(
            a_own[:, :, whole],
            lambda s: lead_own[s, :, whole],
            lambda s: states[s : s + 1, whole],
            lambda rows: y_ref[rows, :],
            lambda rows: gs_ref[rows, :],
            store(y, whole),
            True,
            lambda: pass_own(1, far),
        )

        pass_own(2, far)
        if far > 1:
            for item in range(3):
                pass_own(item, 1)

    def launch_first():
        launch(jnp.zeros((MODES, chans), F32), jnp.zeros((4, chans), F32), jnp.zeros((2, chans), F32))

    pl.when(seq == 0)(launch_first)

    span = float(toks)
    d0, d1, d2 = decay(span), decay(span - 1.0), decay(span - 2.0)
    ahead = z.astype(F32) * span
    a0, a1, a2 = decay(ahead), decay(ahead - 1.0), decay(ahead - 2.0)
    e0, e1, e2 = decay(NZ * span), decay(NZ * span - 1.0), decay(NZ * span - 2.0)

    def send_higher(d):
        pl.semaphore_wait(hello_sem.at[d - 1], 1)
        send_state(d)
        if d == 1:
            send_edge()

    for d in range(1, NZ):
        pl.when(z + d < NZ)(functools.partial(send_higher, d))

    def state_of(n):
        landed(zbuf.at[n], z_r.at[(z - n + NZ - 1) % NZ])

    pl.when(z != 0)(functools.partial(state_of, 0))
    msg = zbuf[0]
    cur, q = msg[:MODES], msg[20:24]
    mine, mine_q = jnp.zeros((MODES, chans), F32), jnp.zeros((4, chans), F32)
    for n in range(1, NZ):
        here = z == n
        mine = jnp.where(here, cur, mine)
        mine_q = jnp.where(here, q, mine_q)
        pl.when(z != n)(functools.partial(state_of, n))
        msg = zbuf[n]
        u0, u1 = edge_tokens(q, msg)
        cur = d0 * cur + msg[:MODES] + d1 * u0 + d2 * u1
        q = msg[20:24]
    tmsg[0:MODES, :] = cur
    tmsg[16:20, :] = zbuf[0, 16:20, :]
    tmsg[20:24, :] = q

    def send_total(d):
        send(tmsg, xbuf.at[x], x_s.at[d - 1], x_r.at[d - 1], (seq + d * NZ, chan))

    for d in range(1, nx):
        pl.when(x + d < nx)(functools.partial(send_total, d))

    gather_first(range(3, half))

    carry[...] = jnp.zeros_like(carry)
    last_q[...] = jnp.zeros_like(last_q)

    def fold(n):
        landed(xbuf.at[n], x_r.at[x - n - 1])
        msg = xbuf[n]
        u0, u1 = edge_tokens(last_q[0:4, :], msg)
        carry[...] = e0 * carry[...] + msg[:MODES] + e1 * u0 + e2 * u1
        last_q[0:4, :] = msg[20:24]

    for n in range(nx - 1):
        pl.when(n < x)(functools.partial(fold, n))
    def rest():
        cur, q = carry[...], last_q[0:4, :]
        u0, u1 = edge_tokens(q, zbuf[0])
        inside = mine + a0 * cur + a1 * u0 + a2 * u1
        at_first = z == 0
        state_in = jnp.where(at_first, cur, inside)
        q = jnp.where(at_first, q, mine_q)
        landed(edge, edge_r.at[0])
        launch(state_in, q, edge[0:2, :])

    pl.when(seq > 0)(rest)

    def slots(dist):
        return sorted({dist, ny - dist}) if dist else [0]

    def first_half(dist):
        for d in slots(dist):
            b = (y + d) % ny
            rebuild(
                a_rep[b] if d else a_own[:, :, 0:LANES],
                (lambda s: lead_rep[b, s]) if d else (lambda s: lead_own[s, :, 0:LANES]),
                lambda s: late[b, s : s + 1, :],
                lambda rows: early[LOCAL, b, rows, :],
                lambda rows: early[GATE, b, rows, :],
                store(b, slice(0, LANES)),
                False,
            )

    def product(dists, of):
        total = None
        for dist in dists:
            for d in slots(dist):
                b = (y + d) % ny
                cols = pl.ds(pl.multiple_of(b * chans, chans), chans)
                term = nt(weight_v[of * rows_w : (of + 1) * rows_w, cols], gathered[b])
                total = term if total is None else total + term
        return total

    def add(dists):
        for of in range(2):
            acc[of] += product(dists, of)

    for b in range(ny):
        own_weights[b].wait()
        landed(held(b, 1), sib_r.at[b])
    first_half(0)
    for of in range(2):
        acc[of] = product([0], of)
    if half == 4:
        arrive(second, 2, (0, 1, 2))
        first_half(2)
        arrive(second, 1, (0, 1, 2))
        first_half(1)
        add([1, 2])
        arrive(second, 3, (0,))
        first_half(3)
        gather_first([4])
        arrive(second, 4, (0,))
        first_half(4)
        arrive(second, 3, (1, 2))
        add([3])
        arrive(second, 4, (1, 2))
        last = [4]
    else:
        gather_first([half])
        for dist in range(1, half + 1):
            arrive(second, dist, (0, 1, 2))
            first_half(dist)
        last = list(range(1, half + 1))
    acc[1] += product(last, 1)
    send(acc.at[1], other_acc, sum_s.at[0], sum_r.at[0], (seq, sibling))
    acc[0] += product(last, 0)
    landed(other_acc, sum_r.at[0])
    acc[0] += other_acc[...]
    out_ref[...] = jnp.dot(acc[0].astype(BF16), perm[...], preferred_element_type=F32).astype(BF16)

    for d in range(1, NZ):
        left(own, z_s.at[d - 1])
    for d in range(1, nx):
        pl.when(x + d < nx)(functools.partial(left, tmsg, x_s.at[d - 1]))
    pl.when(seq < nseq - 1)(functools.partial(left, gate_edge, edge_s.at[0]))
    all_left(first, (GATE, LOCAL))
    all_left(second, (0, 1, 2))
    for b in range(ny):
        left(columns(b, 1 - core), sib_s.at[b])
    left(acc.at[1], sum_s.at[0])


def body(nseq, nchan, gate, key, value, taps, gain, rates, residues, weight):
    chans, toks = gate.shape
    nx, ny = nseq // NZ, nchan // 2
    vmem = pl.BlockSpec(memory_space=pltpu.VMEM)
    anywhere = pl.BlockSpec(memory_space=pl.ANY)
    dma = pltpu.SemaphoreType.DMA
    return pl.pallas_call(
        functools.partial(kernel, nseq, nchan),
        out_shape=pltpu.VMEM((weight.shape[0], toks), BF16),
        in_specs=[anywhere] * 8,
        out_specs=vmem,
        scratch_shapes=[
            pltpu.VMEM(taps.shape, F32),
            pltpu.VMEM((1, chans), F32),
            pltpu.VMEM((MODES, chans), F32),
            pltpu.VMEM((MODES, chans), F32),
            pltpu.VMEM((chans, toks), BF16),
            pltpu.VMEM((chans, toks), BF16),
            pltpu.VMEM((chans, toks), BF16),
            pltpu.VMEM((2 * weight.shape[0], weight.shape[1] // 2), BF16),
            pltpu.VMEM((toks, toks), BF16),
            pltpu.VMEM((toks + 2 * CHUNKS, chans), F32),
            pltpu.VMEM((toks, chans), F32),
            pltpu.VMEM((toks, LANES), F32),
            pltpu.VMEM((toks, LANES), F32),
            pltpu.VMEM((MODES, CHUNKS, chans), F32),
            pltpu.VMEM((NZ, MSG, chans), F32),
            pltpu.VMEM((nx, MSG, chans), F32),
            pltpu.VMEM((MSG, chans), F32),
            pltpu.VMEM((MODES, chans), F32),
            pltpu.VMEM((8, chans), F32),
            pltpu.VMEM((8, chans), F32),
            pltpu.VMEM((8, chans), F32),
            pltpu.VMEM((MODES, chans), F32),
            pltpu.VMEM((MODES, CHUNKS, chans), F32),
            pltpu.VMEM((MODES, CHUNKS, chans), F32),
            pltpu.VMEM((LATE, chans), F32),
            pltpu.VMEM((2, ny, toks, LANES), BF16),
            pltpu.VMEM((ny, 2 * MODES, LANES), F32),
            pltpu.VMEM((ny, LATE, LANES), F32),
            pltpu.VMEM((ny, MODES, CHUNKS, LANES), F32),
            pltpu.VMEM((ny, MODES, CHUNKS, LANES), F32),
            pltpu.VMEM((ny, toks, chans), BF16),
            pltpu.VMEM((2, weight.shape[0], toks), F32),
            pltpu.VMEM((weight.shape[0], toks), F32),
            dma((7,)),
            dma((max(NZ - 1, 1),)),
            dma((max(NZ - 1, 1),)),
            dma((max(nx - 1, 1),)),
            dma((max(nx - 1, 1),)),
            dma((2, ny // 2, 3)),
            dma((2, ny // 2, 3)),
            dma((2, ny // 2, 3)),
            dma((2, ny // 2, 3)),
            dma((ny,)),
            dma((ny,)),
            dma((ny,)),
            dma((1,)),
            dma((1,)),
            dma((1,)),
            dma((1,)),
            pltpu.SemaphoreType.REGULAR((max(NZ - 1, 1),)),
        ],
        compiler_params=pltpu.CompilerParams(
            collective_id=0, has_side_effects=True, vmem_limit_bytes=60 * 1024 * 1024
        ),
        name="hyena",
    )(gate, key, value, taps, gain.reshape(1, -1), rates.T, residues.T, weight)


def solution(mesh):
    in_specs = (
        P("chan", "seq"),
        P("chan", "seq"),
        P("chan", "seq"),
        P(None, "chan"),
        P("chan"),
        P("chan", None),
        P("chan", None),
        P("chan", None),
    )
    return jax.shard_map(
        functools.partial(body, mesh.shape["seq"], mesh.shape["chan"]),
        mesh=mesh,
        in_specs=in_specs,
        out_specs=P("chan", "seq"),
        check_vma=False,
    )
```
